768 devices in a mesh: rows: 48 (over x, z), cols: 16 (over y, core).
Axes of the slice: x: 4, y: 8, z: 12, core: 2. Of those that a mesh axis runs over, the one named last changes fastest.
Arguments:
- features: bfloat16 [98304, 512], P(('rows', 'cols')), may hold values from -6 to 6
- blocks: bfloat16 [48, 512, 128, 128], P('rows', 'cols'), may hold values from -0.15625 to 0.15625
- block_rows: int32 [48, 512], P('rows', 'cols'), may hold values from 0 to 15
- block_cols: int32 [48, 512], P('rows', 'cols'), may hold values from 0 to 6
- block_count: int32 [48, 16], P('rows', 'cols'), may hold values from 1 to 32, as said below
- send_rows: int32 [48, 768, 16], P('rows', 'cols'), may hold values from 0 to 127
Outputs:
- diffused: bfloat16 [98304, 512], P(('rows', 'cols'))
- diffused_two: bfloat16 [98304, 512], P(('rows', 'cols'))
The draws below stay inside these ranges and needn't reach their ends.
Inputs may be any that keep to these rules, and one draw needn't show every extreme that they name: `block_count`: some device has 32 live tiles.
All inputs are finite; a program needn't handle non-finite values.
Results may differ from the reference program's by a relative error of at most 0.025.
Values may be sent and summed in bfloat16 or wider, within the bound.
No kernel may reach another device: no remote copies, remote signals or barrier semaphores. Data moves between devices by JAX's collectives and lax.ppermute only.
A program may use at most 32 MiB of HBM per device.

```python
import jax
import jax.numpy as jnp
from jax import lax

F = 512
BLK = 128
RB = 1
NNZ_DEV = 32
CAP = 16
NODES = 98304
N_ROWS = 48
N_COLS = 16


def draw_block_count(key, part):
    key = jax.random.fold_in(key, 11)
    first, second = jax.random.split(key)
    raw = jax.random.randint(first, (N_ROWS * N_COLS,), 0, NNZ_DEV)
    counts = raw * raw // NNZ_DEV + 1
    chosen = jax.random.randint(second, (), 0, N_ROWS * N_COLS)
    counts = jnp.where(jnp.arange(N_ROWS * N_COLS) == chosen, NNZ_DEV, counts)
    return counts.reshape(N_ROWS, N_COLS).astype(jnp.int32)


def set_ends(values, own_key, smallest, high):
    extent = values.shape
    spot = [jax.random.randint(jax.random.fold_in(own_key, axis), (), 0, extent[axis]) for axis in range(len(extent))]
    values = values.at[tuple(spot)].set(smallest)
    longest = extent.index(max(extent))
    spot[longest] = (spot[longest] + 1) % extent[longest]
    return values.at[tuple(spot)].set(high)


def level_of(key, shape, cuts, low, largest):
    def one(dim, parts):
        draws = jax.random.uniform(jax.random.fold_in(jax.random.fold_in(key, 6), dim), (parts,), jnp.float32, low / len(cuts), largest / len(cuts))
        return jnp.repeat(jnp.exp(draws), shape[dim] // parts).reshape((-1,) + (1,) * (len(shape) - dim - 1))

    loudness = one(*cuts[0])
    for cut in cuts[1:]:
        loudness = loudness * one(*cut)
    return loudness


def gaussian(key, shape, spread, limit, shards=(), kind=jnp.bfloat16):
    gain = level_of(key, shape, shards, -0.22, 0.18) if shards else 1.0
    entries = jax.random.normal(key, shape, jnp.float32) * spread * gain
    return jnp.minimum(jnp.maximum(entries, -limit), limit).astype(kind)


def setup_inputs(seed: int = 0) -> dict:
    keys = jax.random.split(jax.random.key(seed), 7)
    return {
        "features": gaussian(keys[0], (NODES, F), 1.0, 6.0, ((0, 768),)),
        "blocks": gaussian(keys[1], (N_ROWS, N_COLS * NNZ_DEV, BLK, BLK), (BLK * NNZ_DEV // (3 * RB)) ** -0.5, 0.15625, ((0, 48), (1, 16))),
        "block_rows": set_ends(jax.random.randint(keys[2], (N_ROWS, N_COLS * NNZ_DEV), 0, RB * N_COLS), jax.random.fold_in(keys[2], 1), 0, (RB * N_COLS) - 1).astype(jnp.int32),
        "block_cols": set_ends(jax.random.randint(keys[3], (N_ROWS, N_COLS * NNZ_DEV), 0, RB + N_ROWS * CAP // BLK), jax.random.fold_in(keys[3], 1), 0, (RB + N_ROWS * CAP // BLK) - 1).astype(jnp.int32),
        "block_count": draw_block_count(jax.random.fold_in(keys[6], 71), 0),
        "send_rows": set_ends(jax.random.randint(keys[5], (N_ROWS, N_COLS * N_ROWS, CAP), 0, RB * BLK), jax.random.fold_in(keys[5], 1), 0, (RB * BLK) - 1).astype(jnp.int32),
    }


def reference(features, blocks, block_rows, block_cols, block_count, send_rows):
    def hop(feats):
        tiles = feats.reshape(N_ROWS, N_COLS, RB * BLK, F)

        def slab(r):
            def add_column(c, total):
                own = tiles[r, c]
                lists = lax.dynamic_index_in_dim(send_rows, c * N_ROWS + r, 1, keepdims=False)
                column = lax.dynamic_index_in_dim(tiles, c, 1, keepdims=False)
                fetched = jnp.take_along_axis(column, lists[:, :, None], axis=1)
                space = jnp.concatenate([own.reshape(RB, BLK, F), fetched.reshape(-1, BLK, F)], 0).astype(jnp.float32)
                start = (c * NNZ_DEV).astype(jnp.int32)
                tiles_here = lax.dynamic_slice_in_dim(blocks[r], start, NNZ_DEV, 0).astype(jnp.float32)
                rows_here = lax.dynamic_slice_in_dim(block_rows[r], start, NNZ_DEV, 0)
                cols_here = lax.dynamic_slice_in_dim(block_cols[r], start, NNZ_DEV, 0)
                live = (jnp.arange(NNZ_DEV, dtype=jnp.int32) < block_count[r, c]).astype(jnp.float32)
                prods = jnp.einsum('kij,kjf->kif', tiles_here, space[cols_here]) * live[:, None, None]
                select = (rows_here[:, None] == jnp.arange(RB * N_COLS, dtype=jnp.int32)[None, :]).astype(jnp.float32)
                partial_value = jnp.einsum('ks,kif->sif', select, prods)
                rounded = lax.optimization_barrier(partial_value.astype(jnp.bfloat16))
                return total + rounded.astype(jnp.float32)

            empty = jnp.zeros((RB * N_COLS, BLK, F), jnp.float32)
            return lax.fori_loop(0, N_COLS, add_column, empty).astype(jnp.bfloat16)

        result = lax.map(slab, jnp.arange(N_ROWS, dtype=jnp.int32))
        return result.reshape(N_ROWS * N_COLS * RB * BLK, F)

    diffused = hop(features)
    return diffused, hop(diffused)
```

```python
import functools

import jax
import jax.numpy as jnp
from jax import lax
from jax.experimental import pallas as pl
from jax.experimental.pallas import tpu as pltpu
from jax.sharding import Mesh, PartitionSpec as P

GRP = 4
PAIR = [(0, 1), (1, 0)]


def build_kernel(slots, cap, meta_ref, own_ref, other_ref, out_ref, total, spread):
    tile = own_ref.shape[1]
    cells_down, cells_across = total.shape[0], total.shape[1]
    source = lax.broadcasted_iota(jnp.int32, (tile, 2 * tile), 0)
    place = lax.broadcasted_iota(jnp.int32, (tile, 2 * tile), 1)
    for side in range(2):
        plain = side * tile + source
        mixed = (source // cap) * (2 * cap) + side * cap + source % cap
        spread[2 * side] = jnp.where(place == plain, 1.0, 0.0).astype(jnp.bfloat16)
        spread[2 * side + 1] = jnp.where(place == mixed, 1.0, 0.0).astype(jnp.bfloat16)

    def clear(s, carry):
        for t in range(cells_across):
            total[s, t] = jnp.zeros((tile, 2 * tile), jnp.float32)
        return carry

    lax.fori_loop(0, cells_down, clear, 0)
    for side, ref in enumerate((own_ref, other_ref)):
        count = meta_ref[side, 2 * slots]

        def group(index, carry, side=side, ref=ref, count=count):
            found = []
            for step in range(GRP):
                k = index * GRP + step
                col = meta_ref[side, slots + k]
                held = jnp.where(k < count, ref[k], jnp.zeros((tile, tile), ref.dtype))
                kind = 2 * side + jnp.minimum(col, 1)
                moved = jnp.dot(held, spread[kind], preferred_element_type=jnp.float32)
                found.append((meta_ref[side, k], col, moved))
            for row, col, moved in found:
                total[row, col] += moved
            return carry

        lax.fori_loop(0, (count + GRP - 1) // GRP, group, 0)

    def store(s, carry):
        for t in range(cells_across):
            rows = pl.ds(pl.multiple_of(s * tile, tile), tile)
            out_ref[rows, pl.ds(t * 2 * tile, 2 * tile)] = total[s, t].astype(out_ref.dtype)
        return carry

    lax.fori_loop(0, cells_down, store, 0)


def build(meta, own, other, slab_tiles, space_tiles, cap):
    slots, tile = own.shape[0], own.shape[1]
    shape = (slab_tiles * tile, space_tiles * 2 * tile)
    return pl.pallas_call(
        functools.partial(build_kernel, slots, cap),
        out_shape=jax.ShapeDtypeStruct(shape, jnp.bfloat16),
        in_specs=[
            pl.BlockSpec(memory_space=pltpu.SMEM),
            pl.BlockSpec(memory_space=pltpu.VMEM),
            pl.BlockSpec(memory_space=pltpu.VMEM),
        ],
        out_specs=pl.BlockSpec(memory_space=pltpu.VMEM),
        scratch_shapes=[
            pltpu.VMEM((slab_tiles, space_tiles, tile, 2 * tile), jnp.float32),
            pltpu.VMEM((4, tile, 2 * tile), jnp.bfloat16),
        ],
        compiler_params=pltpu.CompilerParams(vmem_limit_bytes=40 * 1024 * 1024),
        cost_estimate=pl.CostEstimate(
            flops=4 * slots * tile * tile * 2 * tile,
            bytes_accessed=8 * shape[0] * shape[1],
            transcendentals=0,
        ),
    )(meta, own, other)


def on_device(features, blocks, block_rows, block_cols, block_count, send_rows):
    held = blocks[0]
    slots, tile = held.shape[0], held.shape[1]
    rows, width = features.shape
    half = width // 2
    cap = send_rows.shape[2]
    owners = lax.axis_size("rows")
    slab_tiles = 2 * lax.axis_size("y")
    space_tiles = 1 + owners * cap // tile
    core = lax.axis_index("core")

    def swap(value):
        return lax.ppermute(value, "core", PAIR)

    low, high = features[:, :half], features[:, half:]
    mine = jnp.where(core == 0, low, high)
    theirs = swap(jnp.where(core == 0, high, low))
    own_field = jnp.concatenate([mine, theirs], 0)

    lists = send_rows[0].reshape(-1)
    numbers = jnp.concatenate([block_rows[0], block_cols[0], block_count[0], lists])
    numbers = jnp.pad(numbers, (0, -numbers.shape[0] % 128))
    both = jnp.stack([numbers, swap(numbers)])
    wanted = both[:, 2 * slots + 1 : 2 * slots + 1 + lists.shape[0]]
    wanted = wanted + jnp.array([[0], [rows]], jnp.int32)
    wanted = wanted.reshape(2, owners, cap).transpose(1, 0, 2).reshape(-1, 1)
    picker = (wanted == lax.broadcasted_iota(jnp.int32, (1, 2 * rows), 1)).astype(jnp.bfloat16)

    meta = both[:, : 2 * slots + 1]
    swapped = lax.broadcasted_iota(jnp.int32, meta.shape, 1) < slots
    meta = jnp.where(swapped, meta ^ core, meta)
    matrix = build(meta, held, swap(held), slab_tiles, space_tiles, cap)

    def hop(field):
        picked = jnp.dot(picker, field, preferred_element_type=jnp.bfloat16)
        fetched = lax.all_to_all(
            picked.reshape(owners, 2 * cap, half), "rows", 0, 0, tiled=True
        )
        space = jnp.concatenate([field, fetched.reshape(-1, half)], 0)
        partial_value = jnp.dot(matrix, space, preferred_element_type=jnp.bfloat16)
        parts = lax.all_to_all(
            partial_value.reshape(-1, 2 * rows, half), "y", 0, 0, tiled=True
        )
        return jnp.sum(parts.astype(jnp.float32), 0).astype(jnp.bfloat16)

    def whole(field):
        kept, other = field[:rows], swap(field[rows:])
        return jnp.concatenate(
            [jnp.where(core == 0, kept, other), jnp.where(core == 0, other, kept)], 1
        )

    first = hop(own_field)
    second = hop(first)
    return (whole(first), whole(second))


def solution(mesh):
    inner = Mesh(
        mesh.devices.reshape(mesh.shape["rows"], -1, 2), ("rows", "y", "core")
    )
    cols = ("y", "core")
    placed = (
        P(("rows", "y", "core"), None),
        P("rows", cols, None, None),
        P("rows", cols),
        P("rows", cols),
        P("rows", cols),
        P("rows", cols, None),
    )
    return jax.shard_map(
        on_device,
        mesh=inner,
        in_specs=placed,
        out_specs=(P(("rows", "y", "core"), None), P(("rows", "y", "core"), None)),
        check_vma=False,
    )
```

```python
import functools

import jax
import jax.numpy as jnp
from jax import lax
from jax.experimental import pallas as pl
from jax.experimental.pallas import tpu as pltpu
from jax.sharding import Mesh, PartitionSpec as P

GRP = 4
STEP_ROWS = 256
PAIR = [(0, 1), (1, 0)]
VMEM_BYTES = 40 * 1024 * 1024


def build_kernel(slots, meta_ref, own_ref, other_ref, out_ref, total):
    tile = own_ref.shape[1]
    cells_down, cells_across = total.shape[0], total.shape[1]

    def clear(s, carry):
        for t in range(cells_across):
            total[s, t] = jnp.zeros((tile, 2 * tile), jnp.float32)
        return carry

    lax.fori_loop(0, cells_down, clear, 0)
    for side, ref in enumerate((own_ref, other_ref)):
        count = meta_ref[side, 2 * slots]
        lanes = pl.ds(side * tile, tile)

        def group(index, carry, side=side, ref=ref, count=count, lanes=lanes):
            for step in range(GRP):
                k = index * GRP + step
                held = jnp.where(k < count, ref[k].astype(jnp.float32), 0.0)
                total[meta_ref[side, k], meta_ref[side, slots + k], :, lanes] += held
            return carry

        lax.fori_loop(0, (count + GRP - 1) // GRP, group, 0)

    def store(s, carry):
        rows = pl.ds(pl.multiple_of(s * tile, tile), tile)
        for t in range(cells_across):
            out_ref[rows, pl.ds(t * 2 * tile, 2 * tile)] = total[s, t].astype(out_ref.dtype)
        return carry

    lax.fori_loop(0, cells_down, store, 0)


def build(meta, own, other, slab_tiles, space_tiles):
    slots, tile = own.shape[0], own.shape[1]
    shape = (slab_tiles * tile, space_tiles * 2 * tile)
    return pl.pallas_call(
        functools.partial(build_kernel, slots),
        out_shape=jax.ShapeDtypeStruct(shape, jnp.bfloat16),
        in_specs=[
            pl.BlockSpec(memory_space=pltpu.SMEM),
            pl.BlockSpec(memory_space=pltpu.VMEM),
            pl.BlockSpec(memory_space=pltpu.VMEM),
        ],
        out_specs=pl.BlockSpec(memory_space=pltpu.VMEM),
        scratch_shapes=[
            pltpu.VMEM((slab_tiles, space_tiles, tile, 2 * tile), jnp.float32),
        ],
        compiler_params=pltpu.CompilerParams(vmem_limit_bytes=VMEM_BYTES),
        cost_estimate=pl.CostEstimate(
            flops=4 * slots * tile * tile,
            bytes_accessed=8 * shape[0] * shape[1],
            transcendentals=0,
        ),
    )(meta, own, other)


def multiply_kernel(cap, matrix_ref, field_ref, *refs):
    *pieces, out_ref, space = refs
    both = field_ref.shape[0]
    tile = both // 2

    @pl.when(pl.program_id(0) == 0)
    def _():
        space[pl.ds(0, both), :] = field_ref[...]
        fetched_tiles = space.shape[0] // both - 1
        if len(pieces) == 2:
            for side, piece in enumerate(pieces):
                for t in range(fetched_tiles):
                    space[pl.ds((t + 1) * both + side * tile, tile), :] = piece[pl.ds(t * tile, tile), :]
        else:
            per_tile = tile // cap
            for owner in range(fetched_tiles * per_tile):
                t, place = divmod(owner, per_tile)
                for side in range(2):
                    space[pl.ds((t + 1) * both + side * tile + place * cap, cap), :] = pieces[0][
                        pl.ds((2 * owner + side) * cap, cap), :
                    ]

    out_ref[...] = jnp.dot(
        matrix_ref[...], space[...], preferred_element_type=jnp.float32
    ).astype(out_ref.dtype)


def multiply(matrix, field, pieces, cap):
    height, depth = matrix.shape
    width = field.shape[1]
    held = [pl.BlockSpec(v.shape, lambda i: (0, 0)) for v in (field, *pieces)]
    return pl.pallas_call(
        functools.partial(multiply_kernel, cap),
        grid=(height // STEP_ROWS,),
        out_shape=jax.ShapeDtypeStruct((height, width), jnp.bfloat16),
        in_specs=[pl.BlockSpec((STEP_ROWS, depth), lambda i: (i, 0)), *held],
        out_specs=pl.BlockSpec((STEP_ROWS, width), lambda i: (i, 0)),
        scratch_shapes=[pltpu.VMEM((depth, width), jnp.bfloat16)],
        compiler_params=pltpu.CompilerParams(vmem_limit_bytes=VMEM_BYTES),
        cost_estimate=pl.CostEstimate(
            flops=2 * height * depth * width,
            bytes_accessed=2 * (height * depth + depth * width + height * width),
            transcendentals=0,
        ),
    )(matrix, field, *pieces)


def one_hot(wanted, extent):
    place = lax.broadcasted_iota(jnp.int32, (1, extent), 1)
    return (wanted.reshape(-1, 1) == place).astype(jnp.bfloat16)


def on_device(features, blocks, block_rows, block_cols, block_count, send_rows):
    held = blocks[0]
    slots, tile = held.shape[0], held.shape[1]
    rows, width = features.shape
    half = width // 2
    cap = send_rows.shape[2]
    owners = lax.axis_size("rows")
    slab_tiles = 2 * lax.axis_size("y")
    space_tiles = 1 + owners * cap // tile
    core = lax.axis_index("core")

    def swap(value):
        return lax.ppermute(value, "core", PAIR)

    def exchange(picked):
        got = lax.all_to_all(picked.reshape(owners, -1, half), "rows", 0, 0, tiled=True)
        return got.reshape(-1, half)

    def pick(chosen, field):
        return jnp.dot(chosen, field, preferred_element_type=jnp.bfloat16)

    low, high = features[:, :half], features[:, half:]
    mine = jnp.where(core == 0, low, high)
    theirs = swap(jnp.where(core == 0, high, low))
    own_field = jnp.concatenate([mine, theirs], 0)

    lists = send_rows[0].reshape(-1)
    numbers = jnp.concatenate([block_rows[0], block_cols[0], block_count[0], lists])
    numbers = jnp.pad(numbers, (0, -numbers.shape[0] % 128))
    both = jnp.stack([numbers, swap(numbers)])
    both_lists = both[:, 2 * slots + 1 : 2 * slots + 1 + lists.shape[0]]
    mixed = both_lists + jnp.array([[0], [rows]], jnp.int32)
    mixed = mixed.reshape(2, owners, cap).transpose(1, 0, 2)
    picker = one_hot(mixed, 2 * rows)

    meta = both[:, : 2 * slots + 1]
    is_row = lax.broadcasted_iota(jnp.int32, meta.shape, 1) < slots
    meta = jnp.where(is_row, meta ^ core, meta)
    other_held = swap(held)

    def in_one(operands):
        own_field, picker, both_lists, meta, held, other_held = operands
        fetched = exchange(pick(picker, own_field))
        matrix = build(meta, held, other_held, slab_tiles, space_tiles)
        return matrix, multiply(matrix, own_field, (fetched,), cap)

    def in_two(operands):
        own_field, picker, both_lists, meta, held, other_held = operands
        pieces = tuple(
            exchange(pick(one_hot(both_lists[side], rows), own_field[side * rows : (side + 1) * rows]))
            for side in range(2)
        )
        matrix = build(meta, held, other_held, slab_tiles, space_tiles)
        return matrix, multiply(matrix, own_field, pieces, cap)

    matrix, partial_value = lax.cond(
        core == 0, in_one, in_two, (own_field, picker, both_lists, meta, held, other_held)
    )

    def combine(partial_value):
        parts = lax.all_to_all(
            partial_value.reshape(-1, 2 * rows, half), "y", 0, 0, tiled=True
        )
        return jnp.sum(parts.astype(jnp.float32), 0).astype(jnp.bfloat16)

    first = combine(partial_value)
    fetched = exchange(pick(picker, first))
    second = combine(multiply(matrix, first, (fetched,), cap))
    others = swap(jnp.stack([first[rows:], second[rows:]])).reshape(2 * rows, half)

    def whole(kept, other):
        return jnp.concatenate(
            [jnp.where(core == 0, kept, other), jnp.where(core == 0, other, kept)], 1
        )

    return (whole(first[:rows], others[:rows]), whole(second[:rows], others[rows:]))


def solution(mesh):
    inner = Mesh(
        mesh.devices.reshape(mesh.shape["rows"], -1, 2), ("rows", "y", "core")
    )
    cols = ("y", "core")
    placed = (
        P(("rows", "y", "core"), None),
        P("rows", cols, None, None),
        P("rows", cols),
        P("rows", cols),
        P("rows", cols),
        P("rows", cols, None),
    )
    return jax.shard_map(
        on_device,
        mesh=inner,
        in_specs=placed,
        out_specs=(P(("rows", "y", "core"), None), P(("rows", "y", "core"), None)),
        check_vma=False,
    )
```

```python
import functools

import jax
import jax.numpy as jnp
from jax import lax
from jax.experimental import pallas as pl
from jax.experimental.pallas import tpu as pltpu
from jax.sharding import Mesh, PartitionSpec as P

GRP = 16
PAIR = [(0, 1), (1, 0)]
VMEM_BYTES = 24 * 1024 * 1024


def product_kernel(slots, cap, meta_ref, own_ref, other_ref, field_ref, *refs):
    *pieces, out_ref, total, space = refs
    tile = own_ref.shape[1]
    tiles = space.shape[0] // 2
    for side in range(2):
        space[side * tiles] = field_ref[pl.ds(side * tile, tile), :]
        for t in range(tiles - 1):
            if len(pieces) == 2:
                space[side * tiles + 1 + t] = pieces[side][pl.ds(t * tile, tile), :]
                continue
            for place in range(tile // cap):
                owner = t * (tile // cap) + place
                space[side * tiles + 1 + t, pl.ds(place * cap, cap), :] = pieces[0][
                    pl.ds((2 * owner + side) * cap, cap), :
                ]
    total[...] = jnp.zeros_like(total)
    for side, ref in enumerate((own_ref, other_ref)):
        count = meta_ref[side, 2 * slots]

        def group(index, carry, side=side, ref=ref, count=count):
            products = []
            for step in range(GRP):
                k = index * GRP + step
                held = jnp.where(k < count, ref[k], jnp.zeros((tile, tile), ref.dtype))
                source = space[side * tiles + meta_ref[side, slots + k]]
                product = jnp.dot(held, source, preferred_element_type=jnp.float32)
                products.append((meta_ref[side, k], product))
            for row, product in products:
                total[row] += product
            return carry

        lax.fori_loop(0, (count + GRP - 1) // GRP, group, 0)
    for row in range(total.shape[0]):
        out_ref[pl.ds(row * tile, tile), :] = total[row].astype(out_ref.dtype)


def product(meta, own, other, field, pieces, slab_tiles, cap):
    slots, tile = own.shape[0], own.shape[1]
    width = field.shape[1]
    tiles = 2 + sum(v.shape[0] for v in pieces) // tile
    anywhere = pl.BlockSpec(memory_space=pltpu.VMEM)
    return pl.pallas_call(
        functools.partial(product_kernel, slots, cap),
        out_shape=jax.ShapeDtypeStruct((slab_tiles * tile, width), jnp.bfloat16),
        in_specs=[pl.BlockSpec(memory_space=pltpu.SMEM)] + [anywhere] * (3 + len(pieces)),
        out_specs=anywhere,
        scratch_shapes=[
            pltpu.VMEM((slab_tiles, tile, width), jnp.float32),
            pltpu.VMEM((tiles, tile, width), jnp.bfloat16),
        ],
        compiler_params=pltpu.CompilerParams(vmem_limit_bytes=VMEM_BYTES),
        cost_estimate=pl.CostEstimate(
            flops=4 * slots * tile * tile * width,
            bytes_accessed=2 * (2 * slots * tile * tile + (tiles + slab_tiles) * tile * width),
            transcendentals=0,
        ),
    )(meta, own, other, field, *pieces)


def one_hot(wanted, extent):
    place = lax.broadcasted_iota(jnp.int32, (1, extent), 1)
    return (wanted.reshape(-1, 1) == place).astype(jnp.bfloat16)


def on_device(features, blocks, block_rows, block_cols, block_count, send_rows):
    held = blocks[0]
    slots, tile = held.shape[0], held.shape[1]
    rows, width = features.shape
    half = width // 2
    cap = send_rows.shape[2]
    owners = lax.axis_size("rows")
    slab_tiles = 2 * lax.axis_size("y")
    core = lax.axis_index("core")

    def swap(value):
        return lax.ppermute(value, "core", PAIR)

    def exchange(picked):
        got = lax.all_to_all(picked.reshape(owners, -1, half), "rows", 0, 0, tiled=True)
        return got.reshape(-1, half)

    def pick(chosen, field):
        return jnp.dot(chosen, field, preferred_element_type=jnp.bfloat16)

    low, high = features[:, :half], features[:, half:]
    mine = jnp.where(core == 0, low, high)
    theirs = swap(jnp.where(core == 0, high, low))
    own_field = jnp.concatenate([mine, theirs], 0)

    lists = send_rows[0].reshape(-1)
    numbers = jnp.concatenate([block_rows[0], block_cols[0], block_count[0], lists])
    numbers = jnp.pad(numbers, (0, -numbers.shape[0] % 128))
    both = jnp.stack([numbers, swap(numbers)])
    both_lists = both[:, 2 * slots + 1 : 2 * slots + 1 + lists.shape[0]]
    mixed = both_lists + jnp.array([[0], [rows]], jnp.int32)
    mixed = mixed.reshape(2, owners, cap).transpose(1, 0, 2).reshape(-1)

    meta = both[:, : 2 * slots + 1]
    is_row = lax.broadcasted_iota(jnp.int32, meta.shape, 1) < slots
    meta = jnp.where(is_row, meta ^ core, meta)
    other_held = swap(held)

    def multiply(field, pieces, meta, held, other_held):
        partial_value = product(meta, held, other_held, field, pieces, slab_tiles, cap)
        parts = lax.all_to_all(
            partial_value.reshape(-1, 2 * rows, half), "y", 0, 0, tiled=True
        )
        return jnp.sum(parts.astype(jnp.float32), 0).astype(jnp.bfloat16)

    def in_one(operands):
        own_field, mixed, both_lists, *tiles = operands
        fetched = exchange(pick(one_hot(mixed, 2 * rows), own_field))
        return multiply(own_field, (fetched,), *tiles)

    def in_two(operands):
        own_field, mixed, both_lists, *tiles = operands
        pieces = tuple(
            exchange(pick(one_hot(both_lists[side], rows), own_field[side * rows : (side + 1) * rows]))
            for side in range(2)
        )
        return multiply(own_field, pieces, *tiles)

    tiles = (meta, held, other_held)
    first = lax.optimization_barrier(
        lax.cond(core == 0, in_one, in_two, (own_field, mixed, both_lists, *tiles))
    )
    fetched = exchange(pick(one_hot(mixed, 2 * rows), first))
    second = multiply(first, (fetched,), *tiles)
    others = swap(jnp.stack([first[rows:], second[rows:]])).reshape(2 * rows, half)

    def whole(kept, other):
        return jnp.concatenate(
            [jnp.where(core == 0, kept, other), jnp.where(core == 0, other, kept)], 1
        )

    return (whole(first[:rows], others[:rows]), whole(second[:rows], others[rows:]))


def solution(mesh):
    inner = Mesh(
        mesh.devices.reshape(mesh.shape["rows"], -1, 2), ("rows", "y", "core")
    )
    cols = ("y", "core")
    placed = (
        P(("rows", "y", "core"), None),
        P("rows", cols, None, None),
        P("rows", cols),
        P("rows", cols),
        P("rows", cols),
        P("rows", cols, None),
    )
    return jax.shard_map(
        on_device,
        mesh=inner,
        in_specs=placed,
        out_specs=(P(("rows", "y", "core"), None), P(("rows", "y", "core"), None)),
        check_vma=False,
    )
```

```python
import functools

import jax
import jax.numpy as jnp
from jax import lax
from jax.experimental import pallas as pl
from jax.experimental.pallas import tpu as pltpu
from jax.sharding import Mesh, PartitionSpec as P

GRP = 16
PAIR = [(0, 1), (1, 0)]
VMEM_BYTES = 24 * 1024 * 1024


def product_kernel(slots, cap, fields, meta_ref, own_ref, other_ref, *refs):
    field, pieces = refs[:fields], refs[fields:-3]
    out_ref, total, space = refs[-3:]
    tile = own_ref.shape[1]
    tiles = space.shape[0] // 2
    for side in range(2):
        if fields == 2:
            space[side * tiles] = field[side][...]
        else:
            space[side * tiles] = field[0][pl.ds(side * tile, tile), :]
        for t in range(tiles - 1):
            if len(pieces) == 2:
                space[side * tiles + 1 + t] = pieces[side][pl.ds(t * tile, tile), :]
                continue
            for place in range(tile // cap):
                owner = t * (tile // cap) + place
                space[side * tiles + 1 + t, pl.ds(place * cap, cap), :] = pieces[0][
                    pl.ds((2 * owner + side) * cap, cap), :
                ]
    total[...] = jnp.zeros_like(total)
    for side, ref in enumerate((own_ref, other_ref)):
        count = meta_ref[side, 2 * slots]

        def group(index, carry, side=side, ref=ref, count=count):
            products = []
            for step in range(GRP):
                k = index * GRP + step
                held = jnp.where(k < count, ref[k], jnp.zeros((tile, tile), ref.dtype))
                source = space[side * tiles + meta_ref[side, slots + k]]
                product = jnp.dot(held, source, preferred_element_type=jnp.float32)
                products.append((meta_ref[side, k], product))
            for row, product in products:
                total[row] += product
            return carry

        lax.fori_loop(0, (count + GRP - 1) // GRP, group, 0)
    for row in range(total.shape[0]):
        out_ref[pl.ds(row * tile, tile), :] = total[row].astype(out_ref.dtype)


def product(meta, own, other, field, pieces, slab_tiles, cap):
    slots, tile = own.shape[0], own.shape[1]
    width = field[0].shape[1]
    tiles = 2 + sum(v.shape[0] for v in pieces) // tile
    anywhere = pl.BlockSpec(memory_space=pltpu.VMEM)
    return pl.pallas_call(
        functools.partial(product_kernel, slots, cap, len(field)),
        out_shape=jax.ShapeDtypeStruct((slab_tiles * tile, width), jnp.bfloat16),
        in_specs=[pl.BlockSpec(memory_space=pltpu.SMEM)] + [anywhere] * (2 + len(field) + len(pieces)),
        out_specs=anywhere,
        scratch_shapes=[
            pltpu.VMEM((slab_tiles, tile, width), jnp.float32),
            pltpu.VMEM((tiles, tile, width), jnp.bfloat16),
        ],
        compiler_params=pltpu.CompilerParams(vmem_limit_bytes=VMEM_BYTES),
        cost_estimate=pl.CostEstimate(
            flops=4 * slots * tile * tile * width,
            bytes_accessed=2 * (2 * slots * tile * tile + (tiles + slab_tiles) * tile * width),
            transcendentals=0,
        ),
    )(meta, own, other, *field, *pieces)


def one_hot(wanted, extent):
    place = lax.broadcasted_iota(jnp.int32, (1, extent), 1)
    return (wanted.reshape(-1, 1) == place).astype(jnp.bfloat16)


def on_device(features, blocks, block_rows, block_cols, block_count, send_rows):
    held = blocks[0]
    slots, tile = held.shape[0], held.shape[1]
    rows, width = features.shape
    half = width // 2
    cap = send_rows.shape[2]
    owners = lax.axis_size("rows")
    slab_tiles = 2 * lax.axis_size("y")
    core = lax.axis_index("core")

    def swap(value):
        return lax.ppermute(value, "core", PAIR)

    def exchange(picked):
        got = lax.all_to_all(picked.reshape(owners, -1, half), "rows", 0, 0, tiled=True)
        return got.reshape(-1, half)

    def pick(chosen, field):
        return jnp.dot(chosen, field, preferred_element_type=jnp.bfloat16)

    low, high = features[:, :half], features[:, half:]
    mine, theirs = jnp.where(core == 0, low, high), jnp.where(core == 0, high, low)
    lists = send_rows[0].reshape(-1)
    every_row = jnp.arange(rows, dtype=jnp.int32)
    numbers = jnp.concatenate([block_rows, block_cols, block_count], 1)
    numbers = jnp.pad(numbers, ((0, cap - 1), (0, half - owners - numbers.shape[1])))
    numbers = jnp.concatenate([send_rows[0].T, numbers], 1)
    sent = pick(one_hot(jnp.concatenate([lists, every_row]), rows), theirs)
    given = swap(jnp.concatenate([sent, numbers.astype(jnp.bfloat16)], 0))
    picked = pick(one_hot(lists, rows), mine)
    other_held = swap(held)
    ends = lists.shape[0], lists.shape[0] + rows

    def places(given, numbers):
        both = jnp.stack([numbers, given[ends[1] :].astype(jnp.int32)])
        meta = both[:, 0, owners : owners + 2 * slots + 1]
        is_row = lax.broadcasted_iota(jnp.int32, meta.shape, 1) < slots
        meta = jnp.where(is_row, meta ^ core, meta)
        wanted = both[:, :, :owners] + jnp.array([[[0]], [[rows]]], jnp.int32)
        return meta, wanted.transpose(2, 0, 1).reshape(-1)

    def multiply(field, pieces, meta, held, other_held):
        partial_value = product(meta, held, other_held, field, pieces, slab_tiles, cap)
        parts = lax.all_to_all(
            partial_value.reshape(-1, 2 * rows, half), "y", 0, 0, tiled=True
        )
        return jnp.sum(parts.astype(jnp.float32), 0).astype(jnp.bfloat16)

    def in_one(operands):
        mine, picked, given, numbers, *tiles = operands
        meta, wanted = places(given, numbers)
        mixed = [v.reshape(owners, cap, half) for v in (picked, given[: ends[0]])]
        fetched = exchange(jnp.concatenate(mixed, 1))
        return multiply((mine, given[ends[0] : ends[1]]), (fetched,), meta, *tiles), meta, wanted

    def in_two(operands):
        mine, picked, given, numbers, *tiles = operands
        meta, wanted = places(given, numbers)
        pieces = exchange(picked), exchange(given[: ends[0]])
        return multiply((mine, given[ends[0] : ends[1]]), pieces, meta, *tiles), meta, wanted

    first, meta, wanted = lax.optimization_barrier(
        lax.cond(core == 0, in_one, in_two, (mine, picked, given, numbers, held, other_held))
    )
    fetched = exchange(pick(one_hot(wanted, 2 * rows), first))
    second = multiply((first,), (fetched,), meta, held, other_held)
    others = swap(jnp.stack([first[rows:], second[rows:]])).reshape(2 * rows, half)

    def whole(kept, other):
        return jnp.concatenate(
            [jnp.where(core == 0, kept, other), jnp.where(core == 0, other, kept)], 1
        )

    return (whole(first[:rows], others[:rows]), whole(second[:rows], others[rows:]))


def solution(mesh):
    inner = Mesh(
        mesh.devices.reshape(mesh.shape["rows"], -1, 2), ("rows", "y", "core")
    )
    cols = ("y", "core")
    placed = (
        P(("rows", "y", "core"), None),
        P("rows", cols, None, None),
        P("rows", cols),
        P("rows", cols),
        P("rows", cols),
        P("rows", cols, None),
    )
    return jax.shard_map(
        on_device,
        mesh=inner,
        in_specs=placed,
        out_specs=(P(("rows", "y", "core"), None), P(("rows", "y", "core"), None)),
        check_vma=False,
    )
```

```python
import functools

import jax
import jax.numpy as jnp
from jax import lax
from jax.experimental import pallas as pl
from jax.experimental.pallas import tpu as pltpu
from jax.sharding import Mesh, PartitionSpec as P

GRP = 16
ALONG_X = 4
PAIR = [(0, 1), (1, 0)]
VMEM_BYTES = 24 * 1024 * 1024


def product_kernel(slots, cap, fields, order, meta_ref, own_ref, other_ref, *refs):
    field = refs[:fields]
    fetched, out_ref, total, space = refs[fields:]
    tile = own_ref.shape[1]
    tiles = space.shape[0] // 2
    for side in range(2):
        if fields == 2:
            space[side * tiles] = field[side][...]
        else:
            space[side * tiles] = field[0][pl.ds(side * tile, tile), :]
        for t in range(tiles - 1):
            for place in range(tile // cap):
                source = 2 * order[t * (tile // cap) + place] + side
                space[side * tiles + 1 + t, pl.ds(place * cap, cap), :] = fetched[
                    pl.ds(source * cap, cap), :
                ]
    total[...] = jnp.zeros_like(total)
    for side, ref in enumerate((own_ref, other_ref)):
        count = meta_ref[side, 2 * slots]

        def group(index, carry, side=side, ref=ref, count=count):
            products = []
            for step in range(GRP):
                k = index * GRP + step
                held = jnp.where(k < count, ref[k], jnp.zeros((tile, tile), ref.dtype))
                source = space[side * tiles + meta_ref[side, slots + k]]
                product = jnp.dot(held, source, preferred_element_type=jnp.float32)
                products.append((meta_ref[side, k], product))
            for row, product in products:
                total[row] += product
            return carry

        lax.fori_loop(0, (count + GRP - 1) // GRP, group, 0)
    for row in range(total.shape[0]):
        out_ref[pl.ds(row * tile, tile), :] = total[row].astype(out_ref.dtype)


def product(meta, own, other, field, fetched, order, slab_tiles, cap):
    slots, tile = own.shape[0], own.shape[1]
    width = field[0].shape[1]
    tiles = 2 + fetched.shape[0] // tile
    anywhere = pl.BlockSpec(memory_space=pltpu.VMEM)
    return pl.pallas_call(
        functools.partial(product_kernel, slots, cap, len(field), order),
        out_shape=jax.ShapeDtypeStruct((slab_tiles * tile, width), jnp.bfloat16),
        in_specs=[pl.BlockSpec(memory_space=pltpu.SMEM)] + [anywhere] * (3 + len(field)),
        out_specs=anywhere,
        scratch_shapes=[
            pltpu.VMEM((slab_tiles, tile, width), jnp.float32),
            pltpu.VMEM((tiles, tile, width), jnp.bfloat16),
        ],
        compiler_params=pltpu.CompilerParams(vmem_limit_bytes=VMEM_BYTES),
        cost_estimate=pl.CostEstimate(
            flops=4 * slots * tile * tile * width,
            bytes_accessed=2 * (2 * slots * tile * tile + (tiles + slab_tiles) * tile * width),
            transcendentals=0,
        ),
    )(meta, own, other, *field, fetched)


def one_hot(wanted, extent):
    place = lax.broadcasted_iota(jnp.int32, (1, extent), 1)
    return (wanted.reshape(-1, 1) == place).astype(jnp.bfloat16)


def on_device(features, blocks, block_rows, block_cols, block_count, send_rows):
    held = blocks[0]
    slots, tile = held.shape[0], held.shape[1]
    rows, width = features.shape
    half = width // 2
    cap = send_rows.shape[2]
    along, across = lax.axis_size("x"), lax.axis_size("z")
    owners = along * across
    slab_tiles = 2 * lax.axis_size("y")
    core = lax.axis_index("core")

    def swap(value):
        return lax.ppermute(value, "core", PAIR)

    def exchange(picked, axes=("x", "z")):
        got = lax.all_to_all(picked.reshape(lax.axis_size(axes), -1, half), axes, 0, 0, tiled=True)
        return got.reshape(-1, half)

    def pick(chosen, field):
        return jnp.dot(chosen, field, preferred_element_type=jnp.bfloat16)

    low, high = features[:, :half], features[:, half:]
    mine, theirs = jnp.where(core == 0, low, high), jnp.where(core == 0, high, low)
    lists = send_rows[0].reshape(-1)
    every_row = jnp.arange(rows, dtype=jnp.int32)
    numbers = jnp.concatenate([block_rows, block_cols, block_count], 1)
    numbers = jnp.pad(numbers, ((0, cap - 1), (0, half - owners - numbers.shape[1])))
    numbers = jnp.concatenate([send_rows[0].T, numbers], 1)
    sent = pick(one_hot(jnp.concatenate([lists, every_row]), rows), theirs)
    given = swap(jnp.concatenate([sent, numbers.astype(jnp.bfloat16)], 0))
    picked = pick(one_hot(lists, rows), mine)
    other_held = swap(held)
    ends = lists.shape[0], lists.shape[0] + rows

    def places(given, numbers):
        both = jnp.stack([numbers, given[ends[1] :].astype(jnp.int32)])
        meta = both[:, 0, owners : owners + 2 * slots + 1]
        is_row = lax.broadcasted_iota(jnp.int32, meta.shape, 1) < slots
        meta = jnp.where(is_row, meta ^ core, meta)
        wanted = both[:, :, :owners] + jnp.array([[[0]], [[rows]]], jnp.int32)
        return meta, wanted.transpose(2, 0, 1).reshape(-1)

    def multiply(field, fetched, order, meta, held, other_held):
        partial_value = product(meta, held, other_held, field, fetched, order, slab_tiles, cap)
        return partial_value.reshape(-1, 2 * rows, half)

    def combine(partial_value):
        parts = lax.all_to_all(partial_value, "y", 0, 0, tiled=True)
        return jnp.sum(parts.astype(jnp.float32), 0).astype(jnp.bfloat16)

    straight = tuple(range(owners))
    turned = tuple(q % across * along + q // across for q in straight)

    def in_one(operands):
        mine, picked, given, numbers, *tiles = operands
        meta, wanted = places(given, numbers)
        mixed = [v.reshape(owners, cap, half) for v in (picked, given[: ends[0]])]
        fetched = exchange(jnp.concatenate(mixed, 1))
        partial_value = multiply((mine, given[ends[0] : ends[1]]), fetched, straight, meta, *tiles)
        partial_value, wanted = lax.optimization_barrier((partial_value, wanted))
        return combine(partial_value), meta, wanted

    def in_steps(operands):
        mine, picked, given, numbers, *tiles = operands
        meta, wanted = places(given, numbers)
        shape = along, across, cap, half
        moved = [exchange(v, "x").reshape(shape) for v in (picked, given[: ends[0]])]
        fetched = exchange(jnp.stack(moved, 2).transpose(1, 0, 2, 3, 4), "z")
        partial_value = multiply((mine, given[ends[0] : ends[1]]), fetched, turned, meta, *tiles)
        partial_value, wanted = lax.optimization_barrier((partial_value, wanted))
        return combine(partial_value), meta, wanted

    first, meta, wanted = lax.optimization_barrier(
        lax.cond(core == 0, in_one, in_steps, (mine, picked, given, numbers, held, other_held))
    )
    fetched = exchange(pick(one_hot(wanted, 2 * rows), first))
    second = combine(multiply((first,), fetched, straight, meta, held, other_held))
    others = swap(jnp.stack([first[rows:], second[rows:]])).reshape(2 * rows, half)

    def whole(kept, other):
        return jnp.concatenate(
            [jnp.where(core == 0, kept, other), jnp.where(core == 0, other, kept)], 1
        )

    return (whole(first[:rows], others[:rows]), whole(second[:rows], others[rows:]))


def solution(mesh):
    inner = Mesh(
        mesh.devices.reshape(ALONG_X, mesh.shape["rows"] // ALONG_X, -1, 2), ("x", "z", "y", "core")
    )
    lines, cols = ("x", "z"), ("y", "core")
    placed = (
        P((*lines, *cols), None),
        P(lines, cols, None, None),
        P(lines, cols),
        P(lines, cols),
        P(lines, cols),
        P(lines, cols, None),
    )
    return jax.shard_map(
        on_device,
        mesh=inner,
        in_specs=placed,
        out_specs=(P((*lines, *cols), None), P((*lines, *cols), None)),
        check_vma=False,
    )
```

```python
import functools

import jax
import jax.numpy as jnp
from jax import lax
from jax.experimental import pallas as pl
from jax.experimental.pallas import tpu as pltpu
from jax.sharding import Mesh, PartitionSpec as P

GRP = 16
ALONG_X = 4
PAIR = [(0, 1), (1, 0)]
VMEM_BYTES = 16 * 1024 * 1024


def product_kernel(slots, cap, fields, order, meta_ref, own_ref, other_ref, *refs):
    field = refs[:fields]
    fetched, out_ref, total, space = refs[fields:]
    tile = own_ref.shape[1]
    tiles = space.shape[0] // 2
    for side in range(2):
        if fields == 2:
            space[side * tiles] = field[side][...]
        else:
            space[side * tiles] = field[0][pl.ds(side * tile, tile), :]
        for t in range(tiles - 1):
            for place in range(tile // cap):
                source = 2 * order[t * (tile // cap) + place] + side
                space[side * tiles + 1 + t, pl.ds(place * cap, cap), :] = fetched[
                    pl.ds(source * cap, cap), :
                ]
    total[...] = jnp.zeros_like(total)
    for side, ref in enumerate((own_ref, other_ref)):
        count = meta_ref[side, 2 * slots]

        def group(index, carry, side=side, ref=ref, count=count):
            products = []
            for step in range(GRP):
                k = index * GRP + step
                held = jnp.where(k < count, ref[k], jnp.zeros((tile, tile), ref.dtype))
                source = space[side * tiles + meta_ref[side, slots + k]]
                product = jnp.dot(held, source, preferred_element_type=jnp.float32)
                products.append((meta_ref[side, k], product))
            for row, product in products:
                total[row] += product
            return carry

        lax.fori_loop(0, (count + GRP - 1) // GRP, group, 0)
    for row in range(total.shape[0]):
        out_ref[pl.ds(row * tile, tile), :] = total[row].astype(out_ref.dtype)


def product(meta, own, other, field, fetched, order, slab_tiles, cap):
    slots, tile = own.shape[0], own.shape[1]
    width = field[0].shape[1]
    tiles = 2 + fetched.shape[0] // tile
    anywhere = pl.BlockSpec(memory_space=pltpu.VMEM)
    return pl.pallas_call(
        functools.partial(product_kernel, slots, cap, len(field), order),
        out_shape=jax.ShapeDtypeStruct((slab_tiles * tile, width), jnp.bfloat16),
        in_specs=[pl.BlockSpec(memory_space=pltpu.SMEM)] + [anywhere] * (3 + len(field)),
        out_specs=anywhere,
        scratch_shapes=[
            pltpu.VMEM((slab_tiles, tile, width), jnp.float32),
            pltpu.VMEM((tiles, tile, width), jnp.bfloat16),
        ],
        compiler_params=pltpu.CompilerParams(vmem_limit_bytes=VMEM_BYTES),
        cost_estimate=pl.CostEstimate(
            flops=4 * slots * tile * tile * width,
            bytes_accessed=2 * (2 * slots * tile * tile + (tiles + slab_tiles) * tile * width),
            transcendentals=0,
        ),
    )(meta, own, other, *field, fetched)


def mix_kernel(cap, mine_ref, given_ref, out_ref):
    for owner in range(mine_ref.shape[0] // cap):
        rows = pl.ds(owner * cap, cap)
        out_ref[pl.ds(2 * owner * cap, cap), :] = mine_ref[rows, :]
        out_ref[pl.ds((2 * owner + 1) * cap, cap), :] = given_ref[rows, :]


def mix(mine, given, cap):
    anywhere = pl.BlockSpec(memory_space=pltpu.VMEM)
    return pl.pallas_call(
        functools.partial(mix_kernel, cap),
        out_shape=jax.ShapeDtypeStruct((2 * mine.shape[0], mine.shape[1]), mine.dtype),
        in_specs=[anywhere, anywhere],
        out_specs=anywhere,
        compiler_params=pltpu.CompilerParams(vmem_limit_bytes=VMEM_BYTES),
    )(mine, given)


def one_hot(wanted, extent):
    place = lax.broadcasted_iota(jnp.int32, (1, extent), 1)
    return (wanted.reshape(-1, 1) == place).astype(jnp.bfloat16)


def on_device(features, blocks, block_rows, block_cols, block_count, send_rows):
    held = blocks[0]
    slots, tile = held.shape[0], held.shape[1]
    rows, width = features.shape
    half = width // 2
    cap = send_rows.shape[2]
    along, across = lax.axis_size("x"), lax.axis_size("z")
    owners = along * across
    slab_tiles = 2 * lax.axis_size("y")
    core = lax.axis_index("core")

    def swap(value):
        return lax.ppermute(value, "core", PAIR)

    def exchange(picked, axes=("x", "z")):
        got = lax.all_to_all(picked.reshape(lax.axis_size(axes), -1, half), axes, 0, 0, tiled=True)
        return got.reshape(-1, half)

    def pick(chosen, field):
        return jnp.dot(chosen, field, preferred_element_type=jnp.bfloat16)

    low, high = features[:, :half], features[:, half:]
    mine, theirs = jnp.where(core == 0, low, high), jnp.where(core == 0, high, low)
    lists = send_rows[0].reshape(-1)
    every_row = jnp.arange(rows, dtype=jnp.int32)
    numbers = jnp.concatenate([block_rows, block_cols, block_count], 1)
    numbers = jnp.pad(numbers, ((0, cap - 1), (0, half - owners - numbers.shape[1])))
    numbers = jnp.concatenate([send_rows[0].T, numbers], 1)
    sent = pick(one_hot(jnp.concatenate([lists, every_row]), rows), theirs)
    given = swap(jnp.concatenate([sent, numbers.astype(jnp.bfloat16)], 0))
    picked = pick(one_hot(lists, rows), mine)
    other_held = swap(held)
    ends = lists.shape[0], lists.shape[0] + rows

    def places(given, numbers):
        both = jnp.stack([numbers, given[ends[1] :].astype(jnp.int32)])
        meta = both[:, 0, owners : owners + 2 * slots + 1]
        is_row = lax.broadcasted_iota(jnp.int32, meta.shape, 1) < slots
        meta = jnp.where(is_row, meta ^ core, meta)
        wanted = both[:, :, :owners] + jnp.array([[[0]], [[rows]]], jnp.int32)
        return meta, wanted.transpose(2, 0, 1).reshape(-1)

    def multiply(field, fetched, order, meta, held, other_held):
        partial_value = product(meta, held, other_held, field, fetched, order, slab_tiles, cap)
        return partial_value.reshape(-1, 2 * rows, half)

    def combine(partial_value):
        parts = lax.all_to_all(partial_value, "y", 0, 0, tiled=True)
        return jnp.sum(parts.astype(jnp.float32), 0).astype(jnp.bfloat16)

    straight = tuple(range(owners))
    turned = tuple(q % across * along + q // across for q in straight)

    def in_one(operands):
        mine, picked, given, numbers, *tiles = operands
        meta, wanted = places(given, numbers)
        fetched = exchange(mix(picked, given, cap))
        partial_value = multiply((mine, given[ends[0] : ends[1]]), fetched, straight, meta, *tiles)
        partial_value, wanted = lax.optimization_barrier((partial_value, wanted))
        return combine(partial_value), meta, wanted

    def in_steps(operands):
        mine, picked, given, numbers, *tiles = operands
        meta, wanted = places(given, numbers)
        meta, wanted, picked, given = lax.optimization_barrier((meta, wanted, picked, given))
        shape = along, across, cap, half
        moved = [exchange(v, "x").reshape(shape) for v in (picked, given[: ends[0]])]
        fetched = exchange(jnp.stack(moved, 2).transpose(1, 0, 2, 3, 4), "z")
        partial_value = multiply((mine, given[ends[0] : ends[1]]), fetched, turned, meta, *tiles)
        partial_value, wanted = lax.optimization_barrier((partial_value, wanted))
        return combine(partial_value), meta, wanted

    first, meta, wanted = lax.optimization_barrier(
        lax.cond(core == 0, in_one, in_steps, (mine, picked, given, numbers, held, other_held))
    )
    fetched = exchange(pick(one_hot(wanted, 2 * rows), first))
    partial_value = multiply((first,), fetched, straight, meta, held, other_held)
    partial_value, first_back = lax.optimization_barrier((partial_value, first[rows:]))
    second = combine(partial_value)
    others = swap(jnp.stack([first_back, second[rows:]])).reshape(2 * rows, half)

    def whole(kept, other):
        return jnp.concatenate(
            [jnp.where(core == 0, kept, other), jnp.where(core == 0, other, kept)], 1
        )

    return (whole(first[:rows], others[:rows]), whole(second[:rows], others[rows:]))


def solution(mesh):
    inner = Mesh(
        mesh.devices.reshape(ALONG_X, mesh.shape["rows"] // ALONG_X, -1, 2), ("x", "z", "y", "core")
    )
    lines, cols = ("x", "z"), ("y", "core")
    placed = (
        P((*lines, *cols), None),
        P(lines, cols, None, None),
        P(lines, cols),
        P(lines, cols),
        P(lines, cols),
        P(lines, cols, None),
    )
    return jax.shard_map(
        on_device,
        mesh=inner,
        in_specs=placed,
        out_specs=(P((*lines, *cols), None), P((*lines, *cols), None)),
        check_vma=False,
    )
```

```python
import functools

import jax
import jax.numpy as jnp
from jax import lax
from jax.experimental import pallas as pl
from jax.experimental.pallas import tpu as pltpu
from jax.sharding import Mesh, PartitionSpec as P

GRP = 16
PAIR = [(0, 1), (1, 0)]
VMEM_BYTES = 16 * 1024 * 1024


def product_kernel(slots, cap, fields, meta_ref, own_ref, other_ref, *refs):
    starts = fields
    field, fetched = refs[: len(starts)], refs[len(starts) : -3]
    out_ref, total, space = refs[-3:]
    tile = own_ref.shape[1]
    tiles = space.shape[0] // 2
    for side in range(2):
        if len(field) == 2:
            space[side * tiles] = field[side][pl.ds(starts[side], tile), :]
        else:
            space[side * tiles] = field[0][pl.ds(side * tile, tile), :]
        for t in range(tiles - 1):
            if len(fetched) == 2:
                space[side * tiles + 1 + t] = fetched[side][pl.ds(t * tile, tile), :]
                continue
            for place in range(tile // cap):
                source = 2 * (t * (tile // cap) + place) + side
                space[side * tiles + 1 + t, pl.ds(place * cap, cap), :] = fetched[0][
                    pl.ds(source * cap, cap), :
                ]
    total[...] = jnp.zeros_like(total)
    for side, ref in enumerate((own_ref, other_ref)):
        count = meta_ref[side, 2 * slots]

        def group(index, carry, side=side, ref=ref, count=count):
            products = []
            for step in range(GRP):
                k = index * GRP + step
                held = jnp.where(k < count, ref[k], jnp.zeros((tile, tile), ref.dtype))
                source = space[side * tiles + meta_ref[side, slots + k]]
                product = jnp.dot(held, source, preferred_element_type=jnp.float32)
                products.append((meta_ref[side, k], product))
            for row, product in products:
                total[row] += product
            return carry

        lax.fori_loop(0, (count + GRP - 1) // GRP, group, 0)
    for row in range(total.shape[0]):
        out_ref[pl.ds(row * tile, tile), :] = total[row].astype(out_ref.dtype)


def product(meta, own, other, field, starts, fetched, slab_tiles, cap):
    slots, tile = own.shape[0], own.shape[1]
    width = field[0].shape[1]
    tiles = 2 + sum(v.shape[0] for v in fetched) // tile
    anywhere = pl.BlockSpec(memory_space=pltpu.VMEM)
    return pl.pallas_call(
        functools.partial(product_kernel, slots, cap, starts),
        out_shape=jax.ShapeDtypeStruct((slab_tiles * tile, width), jnp.bfloat16),
        in_specs=[pl.BlockSpec(memory_space=pltpu.SMEM)] + [anywhere] * (2 + len(field) + len(fetched)),
        out_specs=anywhere,
        scratch_shapes=[
            pltpu.VMEM((slab_tiles, tile, width), jnp.float32),
            pltpu.VMEM((tiles, tile, width), jnp.bfloat16),
        ],
        compiler_params=pltpu.CompilerParams(vmem_limit_bytes=VMEM_BYTES),
        cost_estimate=pl.CostEstimate(
            flops=4 * slots * tile * tile * width,
            bytes_accessed=2 * (2 * slots * tile * tile + (tiles + slab_tiles) * tile * width),
            transcendentals=0,
        ),
    )(meta, own, other, *field, *fetched)


def mix_kernel(cap, mine_ref, given_ref, out_ref):
    for owner in range(mine_ref.shape[0] // cap):
        rows = pl.ds(owner * cap, cap)
        out_ref[pl.ds(2 * owner * cap, cap), :] = mine_ref[rows, :]
        out_ref[pl.ds((2 * owner + 1) * cap, cap), :] = given_ref[rows, :]


def mix(mine, given, cap):
    anywhere = pl.BlockSpec(memory_space=pltpu.VMEM)
    return pl.pallas_call(
        functools.partial(mix_kernel, cap),
        out_shape=jax.ShapeDtypeStruct((2 * mine.shape[0], mine.shape[1]), mine.dtype),
        in_specs=[anywhere, anywhere],
        out_specs=anywhere,
        compiler_params=pltpu.CompilerParams(vmem_limit_bytes=VMEM_BYTES),
    )(mine, given)


def pick_kernel(core_ref, features_ref, lists_ref, rows_ref, cols_ref, count_ref, mine_ref, sent_ref, chosen, numbers):
    cap, owners = lists_ref.shape
    rows, half = features_ref.shape[0], mine_ref.shape[1]
    place = lax.broadcasted_iota(jnp.int32, (cap, rows), 1)
    for owner in range(owners):
        wanted = lists_ref[:, pl.ds(owner, 1)]
        chosen[pl.ds(owner * cap, cap), :] = jnp.where(wanted == place, 1.0, 0.0).astype(chosen.dtype)
    core = core_ref[0]
    mine = features_ref[:, pl.ds(pl.multiple_of(core * half, half), half)]
    theirs = features_ref[:, pl.ds(pl.multiple_of((1 - core) * half, half), half)]
    ends = mine_ref.shape[0], mine_ref.shape[0] + rows
    sent_ref[pl.ds(0, ends[0]), :] = jnp.dot(
        chosen[...], theirs, preferred_element_type=jnp.float32
    ).astype(sent_ref.dtype)
    sent_ref[pl.ds(ends[0], rows), :] = theirs
    numbers[...] = jnp.zeros_like(numbers)
    numbers[:, pl.ds(0, owners)] = lists_ref[...]
    slots = rows_ref.shape[1]
    numbers[pl.ds(0, 1), pl.ds(rows, slots)] = rows_ref[...]
    numbers[pl.ds(1, 1), pl.ds(rows, slots)] = cols_ref[...]
    numbers[pl.ds(2, 1), pl.ds(rows, 1)] = count_ref[...]
    sent_ref[pl.ds(ends[1], cap), :] = numbers[...].astype(jnp.float32).astype(sent_ref.dtype)
    mine_ref[...] = jnp.dot(chosen[...], mine, preferred_element_type=jnp.float32).astype(mine_ref.dtype)


def pick_own(core, features, lists, block_rows, block_cols, block_count):
    cap, owners = lists.shape
    rows, half = features.shape[0], features.shape[1] // 2
    anywhere = pl.BlockSpec(memory_space=pltpu.VMEM)
    return pl.pallas_call(
        pick_kernel,
        out_shape=(
            jax.ShapeDtypeStruct((owners * cap, half), features.dtype),
            jax.ShapeDtypeStruct((owners * cap + rows + cap, half), features.dtype),
        ),
        in_specs=[pl.BlockSpec(memory_space=pltpu.SMEM)] + [anywhere] * 5,
        out_specs=(anywhere, anywhere),
        scratch_shapes=[
            pltpu.VMEM((owners * cap, rows), jnp.bfloat16),
            pltpu.VMEM((cap, half), jnp.int32),
        ],
        compiler_params=pltpu.CompilerParams(vmem_limit_bytes=VMEM_BYTES),
    )(core.reshape(1), features, lists, block_rows, block_cols, block_count)


def one_hot(wanted, extent):
    place = lax.broadcasted_iota(jnp.int32, (1, extent), 1)
    return (wanted.reshape(-1, 1) == place).astype(jnp.bfloat16)


def on_device(features, blocks, block_rows, block_cols, block_count, send_rows):
    held = blocks[0]
    slots, tile = held.shape[0], held.shape[1]
    rows, width = features.shape
    half = width // 2
    cap = send_rows.shape[2]
    owners = lax.axis_size("rows")
    slab_tiles = 2 * lax.axis_size("y")
    core = lax.axis_index("core")

    def swap(value):
        return lax.ppermute(value, "core", PAIR)

    def exchange(picked):
        got = lax.all_to_all(picked.reshape(owners, -1, half), "rows", 0, 0, tiled=True)
        return got.reshape(-1, half)

    def pick(chosen, field):
        return jnp.dot(chosen, field, preferred_element_type=jnp.bfloat16)

    other_held = swap(held)
    lists = send_rows[0].T
    picked, sent = pick_own(core, features, lists, block_rows, block_cols, block_count)
    given = swap(sent)
    mine = jnp.where(core == 0, features[:, :half], features[:, half:])
    ends = owners * cap, owners * cap + rows

    def places(given):
        numbers = given[ends[1] :].astype(jnp.int32)
        other = [numbers[:1, rows : rows + slots], numbers[1:2, rows : rows + slots], numbers[2:3, rows : rows + 1]]
        meta = jnp.concatenate([jnp.concatenate([block_rows, block_cols, block_count], 1), jnp.concatenate(other, 1)], 0)
        is_row = lax.broadcasted_iota(jnp.int32, meta.shape, 1) < slots
        meta = jnp.where(is_row, meta ^ core, meta)
        wanted = jnp.stack([lists, numbers[:, :owners] + rows])
        return meta, wanted.transpose(2, 0, 1).reshape(-1)

    def multiply(field, starts, fetched, meta, held, other_held):
        partial_value = product(meta, held, other_held, field, starts, fetched, slab_tiles, cap)
        return partial_value.reshape(-1, 2 * rows, half)

    def combine(partial_value):
        parts = lax.all_to_all(partial_value, "y", 0, 0, tiled=True)
        return jnp.sum(parts.astype(jnp.float32), 0).astype(jnp.bfloat16)

    def in_one(operands):
        mine, picked, given, *tiles = operands
        meta, wanted = places(given)
        meta, wanted, picked, given, mine = lax.optimization_barrier((meta, wanted, picked, given, mine))
        fetched = exchange(mix(picked, given, cap))
        partial_value = multiply((mine, given), (0, ends[0]), (fetched,), meta, *tiles)
        return combine(partial_value), meta, wanted

    def in_two(operands):
        mine, picked, given, *tiles = operands
        meta, wanted = places(given)
        pieces = exchange(picked), exchange(given[: ends[0]])
        partial_value = multiply((mine, given), (0, ends[0]), pieces, meta, *tiles)
        partial_value, wanted = lax.optimization_barrier((partial_value, wanted))
        return combine(partial_value), meta, wanted

    first, meta, wanted = lax.optimization_barrier(
        lax.cond(core == 0, in_one, in_two, (mine, picked, given, held, other_held))
    )
    fetched = exchange(pick(one_hot(wanted, 2 * rows), first))
    partial_value = multiply((first,), (0,), (fetched,), meta, held, other_held)
    partial_value, first_back = lax.optimization_barrier((partial_value, first[rows:]))
    second = combine(partial_value)
    others = swap(jnp.stack([first_back, second[rows:]])).reshape(2 * rows, half)

    def whole(kept, other):
        return jnp.concatenate(
            [jnp.where(core == 0, kept, other), jnp.where(core == 0, other, kept)], 1
        )

    return (whole(first[:rows], others[:rows]), whole(second[:rows], others[rows:]))


def solution(mesh):
    inner = Mesh(
        mesh.devices.reshape(mesh.shape["rows"], -1, 2), ("rows", "y", "core")
    )
    cols = ("y", "core")
    placed = (
        P(("rows", "y", "core"), None),
        P("rows", cols, None, None),
        P("rows", cols),
        P("rows", cols),
        P("rows", cols),
        P("rows", cols, None),
    )
    return jax.shard_map(
        on_device,
        mesh=inner,
        in_specs=placed,
        out_specs=(P(("rows", "y", "core"), None), P(("rows", "y", "core"), None)),
        check_vma=False,
    )
```

```python
import functools

import jax
import jax.numpy as jnp
from jax import lax
from jax.experimental import pallas as pl
from jax.experimental.pallas import tpu as pltpu
from jax.sharding import Mesh, PartitionSpec as P

GRP = 16
ALONG_X = 4
PAIR = [(0, 1), (1, 0)]
VMEM_BYTES = 16 * 1024 * 1024


def product_kernel(slots, cap, starts, order, meta_ref, own_ref, other_ref, *refs):
    field = refs[: len(starts)]
    fetched, out_ref, total, space = refs[len(starts) :]
    tile = own_ref.shape[1]
    tiles = space.shape[0] // 2
    for side in range(2):
        if len(field) == 2:
            space[side * tiles] = field[side][pl.ds(starts[side], tile), :]
        else:
            space[side * tiles] = field[0][pl.ds(side * tile, tile), :]
        for t in range(tiles - 1):
            for place in range(tile // cap):
                source = 2 * order[t * (tile // cap) + place] + side
                space[side * tiles + 1 + t, pl.ds(place * cap, cap), :] = fetched[
                    pl.ds(source * cap, cap), :
                ]
    total[...] = jnp.zeros_like(total)
    for side, ref in enumerate((own_ref, other_ref)):
        count = meta_ref[side, 2 * slots]

        def group(index, carry, side=side, ref=ref, count=count):
            products = []
            for step in range(GRP):
                k = index * GRP + step
                held = jnp.where(k < count, ref[k], jnp.zeros((tile, tile), ref.dtype))
                source = space[side * tiles + meta_ref[side, slots + k]]
                product = jnp.dot(held, source, preferred_element_type=jnp.float32)
                products.append((meta_ref[side, k], product))
            for row, product in products:
                total[row] += product
            return carry

        lax.fori_loop(0, (count + GRP - 1) // GRP, group, 0)
    for row in range(total.shape[0]):
        out_ref[pl.ds(row * tile, tile), :] = total[row].astype(out_ref.dtype)


def product(meta, own, other, field, starts, fetched, order, slab_tiles, cap):
    slots, tile = own.shape[0], own.shape[1]
    width = field[0].shape[1]
    tiles = 2 + fetched.shape[0] // tile
    anywhere = pl.BlockSpec(memory_space=pltpu.VMEM)
    return pl.pallas_call(
        functools.partial(product_kernel, slots, cap, starts, order),
        out_shape=jax.ShapeDtypeStruct((slab_tiles * tile, width), jnp.bfloat16),
        in_specs=[pl.BlockSpec(memory_space=pltpu.SMEM)] + [anywhere] * (3 + len(field)),
        out_specs=anywhere,
        scratch_shapes=[
            pltpu.VMEM((slab_tiles, tile, width), jnp.float32),
            pltpu.VMEM((tiles, tile, width), jnp.bfloat16),
        ],
        compiler_params=pltpu.CompilerParams(vmem_limit_bytes=VMEM_BYTES),
        cost_estimate=pl.CostEstimate(
            flops=4 * slots * tile * tile * width,
            bytes_accessed=2 * (2 * slots * tile * tile + (tiles + slab_tiles) * tile * width),
            transcendentals=0,
        ),
    )(meta, own, other, *field, fetched)


def mix_kernel(cap, mine_ref, given_ref, out_ref):
    for owner in range(mine_ref.shape[0] // cap):
        rows = pl.ds(owner * cap, cap)
        out_ref[pl.ds(2 * owner * cap, cap), :] = mine_ref[rows, :]
        out_ref[pl.ds((2 * owner + 1) * cap, cap), :] = given_ref[rows, :]


def mix(mine, given, cap):
    anywhere = pl.BlockSpec(memory_space=pltpu.VMEM)
    return pl.pallas_call(
        functools.partial(mix_kernel, cap),
        out_shape=jax.ShapeDtypeStruct((2 * mine.shape[0], mine.shape[1]), mine.dtype),
        in_specs=[anywhere, anywhere],
        out_specs=anywhere,
        compiler_params=pltpu.CompilerParams(vmem_limit_bytes=VMEM_BYTES),
    )(mine, given)


def pick_kernel(core_ref, features_ref, lists_ref, rows_ref, cols_ref, count_ref, mine_ref, sent_ref, chosen, numbers):
    cap, owners = lists_ref.shape
    rows, half = features_ref.shape[0], mine_ref.shape[1]
    place = lax.broadcasted_iota(jnp.int32, (cap, rows), 1)
    for owner in range(owners):
        wanted = lists_ref[:, pl.ds(owner, 1)]
        chosen[pl.ds(owner * cap, cap), :] = jnp.where(wanted == place, 1.0, 0.0).astype(chosen.dtype)
    core = core_ref[0]
    mine = features_ref[:, pl.ds(pl.multiple_of(core * half, half), half)]
    theirs = features_ref[:, pl.ds(pl.multiple_of((1 - core) * half, half), half)]
    ends = mine_ref.shape[0], mine_ref.shape[0] + rows
    sent_ref[pl.ds(0, ends[0]), :] = jnp.dot(
        chosen[...], theirs, preferred_element_type=jnp.float32
    ).astype(sent_ref.dtype)
    sent_ref[pl.ds(ends[0], rows), :] = theirs
    numbers[...] = jnp.zeros_like(numbers)
    numbers[:, pl.ds(0, owners)] = lists_ref[...]
    slots = rows_ref.shape[1]
    numbers[pl.ds(0, 1), pl.ds(rows, slots)] = rows_ref[...]
    numbers[pl.ds(1, 1), pl.ds(rows, slots)] = cols_ref[...]
    numbers[pl.ds(2, 1), pl.ds(rows, 1)] = count_ref[...]
    sent_ref[pl.ds(ends[1], cap), :] = numbers[...].astype(jnp.float32).astype(sent_ref.dtype)
    mine_ref[...] = jnp.dot(chosen[...], mine, preferred_element_type=jnp.float32).astype(mine_ref.dtype)


def pick_own(core, features, lists, block_rows, block_cols, block_count):
    cap, owners = lists.shape
    rows, half = features.shape[0], features.shape[1] // 2
    anywhere = pl.BlockSpec(memory_space=pltpu.VMEM)
    return pl.pallas_call(
        pick_kernel,
        out_shape=(
            jax.ShapeDtypeStruct((owners * cap, half), features.dtype),
            jax.ShapeDtypeStruct((owners * cap + rows + cap, half), features.dtype),
        ),
        in_specs=[pl.BlockSpec(memory_space=pltpu.SMEM)] + [anywhere] * 5,
        out_specs=(anywhere, anywhere),
        scratch_shapes=[
            pltpu.VMEM((owners * cap, rows), jnp.bfloat16),
            pltpu.VMEM((cap, half), jnp.int32),
        ],
        compiler_params=pltpu.CompilerParams(vmem_limit_bytes=VMEM_BYTES),
    )(core.reshape(1), features, lists, block_rows, block_cols, block_count)


def one_hot(wanted, extent):
    place = lax.broadcasted_iota(jnp.int32, (1, extent), 1)
    return (wanted.reshape(-1, 1) == place).astype(jnp.bfloat16)


def on_device(features, blocks, block_rows, block_cols, block_count, send_rows):
    held = blocks[0]
    slots, tile = held.shape[0], held.shape[1]
    rows, width = features.shape
    half = width // 2
    cap = send_rows.shape[2]
    along, across = lax.axis_size("x"), lax.axis_size("z")
    owners = along * across
    slab_tiles = 2 * lax.axis_size("y")
    core = lax.axis_index("core")

    def swap(value):
        return lax.ppermute(value, "core", PAIR)

    def exchange(picked, axes=("x", "z")):
        got = lax.all_to_all(picked.reshape(lax.axis_size(axes), -1, half), axes, 0, 0, tiled=True)
        return got.reshape(-1, half)

    def pick(chosen, field):
        return jnp.dot(chosen, field, preferred_element_type=jnp.bfloat16)

    other_held = swap(held)
    lists = send_rows[0].T
    picked, sent = pick_own(core, features, lists, block_rows, block_cols, block_count)
    given = swap(sent)
    mine = jnp.where(core == 0, features[:, :half], features[:, half:])
    ends = owners * cap, owners * cap + rows

    def places(given):
        numbers = given[ends[1] :].astype(jnp.int32)
        other = [numbers[:1, rows : rows + slots], numbers[1:2, rows : rows + slots], numbers[2:3, rows : rows + 1]]
        meta = jnp.concatenate([jnp.concatenate([block_rows, block_cols, block_count], 1), jnp.concatenate(other, 1)], 0)
        is_row = lax.broadcasted_iota(jnp.int32, meta.shape, 1) < slots
        meta = jnp.where(is_row, meta ^ core, meta)
        wanted = jnp.stack([lists, numbers[:, :owners] + rows])
        return meta, wanted.transpose(2, 0, 1).reshape(-1)

    def multiply(field, starts, fetched, order, meta, held, other_held):
        partial_value = product(meta, held, other_held, field, starts, fetched, order, slab_tiles, cap)
        return partial_value.reshape(-1, 2 * rows, half)

    def combine(partial_value):
        parts = lax.all_to_all(partial_value, "y", 0, 0, tiled=True)
        return jnp.sum(parts.astype(jnp.float32), 0).astype(jnp.bfloat16)

    straight = tuple(range(owners))
    turned = tuple(q % across * along + q // across for q in straight)

    def in_one(operands):
        mine, picked, given, *tiles = operands
        meta, wanted = places(given)
        fetched = exchange(mix(picked, given, cap))
        partial_value = multiply((mine, given), (0, ends[0]), fetched, straight, meta, *tiles)
        partial_value, wanted = lax.optimization_barrier((partial_value, wanted))
        return combine(partial_value), meta, wanted

    def in_steps(operands):
        mine, picked, given, *tiles = operands
        meta, wanted = places(given)
        meta, wanted, picked, given = lax.optimization_barrier((meta, wanted, picked, given))
        shape = along, across, cap, half
        moved = [exchange(v, "x").reshape(shape) for v in (picked, given[: ends[0]])]
        fetched = exchange(jnp.stack(moved, 2).transpose(1, 0, 2, 3, 4), "z")
        partial_value = multiply((mine, given), (0, ends[0]), fetched, turned, meta, *tiles)
        return combine(partial_value), meta, wanted

    first, meta, wanted = lax.optimization_barrier(
        lax.cond(core == 0, in_one, in_steps, (mine, picked, given, held, other_held))
    )
    fetched = exchange(pick(one_hot(wanted, 2 * rows), first))
    second = combine(multiply((first,), (0,), fetched, straight, meta, held, other_held))
    kept_back = lax.optimization_barrier((first, second))
    others = swap(jnp.stack([v[rows:] for v in kept_back])).reshape(2 * rows, half)

    def whole(kept, other):
        return jnp.concatenate(
            [jnp.where(core == 0, kept, other), jnp.where(core == 0, other, kept)], 1
        )

    return (whole(first[:rows], others[:rows]), whole(second[:rows], others[rows:]))


def solution(mesh):
    inner = Mesh(
        mesh.devices.reshape(ALONG_X, mesh.shape["rows"] // ALONG_X, -1, 2), ("x", "z", "y", "core")
    )
    lines, cols = ("x", "z"), ("y", "core")
    placed = (
        P((*lines, *cols), None),
        P(lines, cols, None, None),
        P(lines, cols),
        P(lines, cols),
        P(lines, cols),
        P(lines, cols, None),
    )
    return jax.shard_map(
        on_device,
        mesh=inner,
        in_specs=placed,
        out_specs=(P((*lines, *cols), None), P((*lines, *cols), None)),
        check_vma=False,
    )
```

```python
import functools

import jax
import jax.numpy as jnp
from jax import lax
from jax.experimental import pallas as pl
from jax.experimental.pallas import tpu as pltpu
from jax.sharding import Mesh, PartitionSpec as P

GRP = 32
ALONG_X = 4
PAIR = [(0, 1), (1, 0)]
VMEM_BYTES = 16 * 1024 * 1024


def product_kernel(slots, cap, starts, order, meta_ref, own_ref, other_ref, *refs):
    field = refs[: len(starts)]
    fetched, out_ref, total, space = refs[len(starts) :]
    tile = own_ref.shape[1]
    tiles = space.shape[0] // 2
    for side in range(2):
        if len(field) == 2:
            space[side * tiles] = field[side][pl.ds(starts[side], tile), :]
        else:
            space[side * tiles] = field[0][pl.ds(side * tile, tile), :]
        for t in range(tiles - 1):
            for place in range(tile // cap):
                source = 2 * order[t * (tile // cap) + place] + side
                space[side * tiles + 1 + t, pl.ds(place * cap, cap), :] = fetched[
                    pl.ds(source * cap, cap), :
                ]
    total[...] = jnp.zeros_like(total)
    for side, ref in enumerate((own_ref, other_ref)):
        count = meta_ref[side, 2 * slots]

        def group(index, carry, side=side, ref=ref, count=count):
            products = []
            for step in range(GRP):
                k = index * GRP + step
                held = jnp.where(k < count, ref[k], jnp.zeros((tile, tile), ref.dtype))
                source = space[side * tiles + meta_ref[side, slots + k]]
                product = jnp.dot(held, source, preferred_element_type=jnp.float32)
                products.append((meta_ref[side, k], product))
            for row, product in products:
                total[row] += product
            return carry

        lax.fori_loop(0, (count + GRP - 1) // GRP, group, 0)
    for row in range(total.shape[0]):
        out_ref[pl.ds(row * tile, tile), :] = total[row].astype(out_ref.dtype)


def product(meta, own, other, field, starts, fetched, order, slab_tiles, cap):
    slots, tile = own.shape[0], own.shape[1]
    width = field[0].shape[1]
    tiles = 2 + fetched.shape[0] // tile
    anywhere = pl.BlockSpec(memory_space=pltpu.VMEM)
    return pl.pallas_call(
        functools.partial(product_kernel, slots, cap, starts, order),
        out_shape=jax.ShapeDtypeStruct((slab_tiles * tile, width), jnp.bfloat16),
        in_specs=[pl.BlockSpec(memory_space=pltpu.SMEM)] + [anywhere] * (3 + len(field)),
        out_specs=anywhere,
        scratch_shapes=[
            pltpu.VMEM((slab_tiles, tile, width), jnp.float32),
            pltpu.VMEM((tiles, tile, width), jnp.bfloat16),
        ],
        compiler_params=pltpu.CompilerParams(vmem_limit_bytes=VMEM_BYTES),
        cost_estimate=pl.CostEstimate(
            flops=4 * slots * tile * tile * width,
            bytes_accessed=2 * (2 * slots * tile * tile + (tiles + slab_tiles) * tile * width),
            transcendentals=0,
        ),
    )(meta, own, other, *field, fetched)


def mix_kernel(cap, mine_ref, given_ref, out_ref):
    for owner in range(mine_ref.shape[0] // cap):
        rows = pl.ds(owner * cap, cap)
        out_ref[pl.ds(2 * owner * cap, cap), :] = mine_ref[rows, :]
        out_ref[pl.ds((2 * owner + 1) * cap, cap), :] = given_ref[rows, :]


def mix(mine, given, cap):
    anywhere = pl.BlockSpec(memory_space=pltpu.VMEM)
    return pl.pallas_call(
        functools.partial(mix_kernel, cap),
        out_shape=jax.ShapeDtypeStruct((2 * mine.shape[0], mine.shape[1]), mine.dtype),
        in_specs=[anywhere, anywhere],
        out_specs=anywhere,
        compiler_params=pltpu.CompilerParams(vmem_limit_bytes=VMEM_BYTES),
    )(mine, given)


def pick_kernel(core_ref, features_ref, lists_ref, rows_ref, cols_ref, count_ref, mine_ref, sent_ref, chosen, numbers):
    cap, owners = lists_ref.shape
    rows, half = features_ref.shape[0], mine_ref.shape[1]
    place = lax.broadcasted_iota(jnp.int32, (cap, rows), 1)
    for owner in range(owners):
        wanted = lists_ref[:, pl.ds(owner, 1)]
        chosen[pl.ds(owner * cap, cap), :] = jnp.where(wanted == place, 1.0, 0.0).astype(chosen.dtype)
    core = core_ref[0]
    mine = features_ref[:, pl.ds(pl.multiple_of(core * half, half), half)]
    theirs = features_ref[:, pl.ds(pl.multiple_of((1 - core) * half, half), half)]
    ends = mine_ref.shape[0], mine_ref.shape[0] + rows
    sent_ref[pl.ds(0, ends[0]), :] = jnp.dot(
        chosen[...], theirs, preferred_element_type=jnp.float32
    ).astype(sent_ref.dtype)
    sent_ref[pl.ds(ends[0], rows), :] = theirs
    numbers[...] = jnp.zeros_like(numbers)
    numbers[:, pl.ds(0, owners)] = lists_ref[...]
    slots = rows_ref.shape[1]
    numbers[pl.ds(0, 1), pl.ds(rows, slots)] = rows_ref[...]
    numbers[pl.ds(1, 1), pl.ds(rows, slots)] = cols_ref[...]
    numbers[pl.ds(2, 1), pl.ds(rows, 1)] = count_ref[...]
    sent_ref[pl.ds(ends[1], cap), :] = numbers[...].astype(jnp.float32).astype(sent_ref.dtype)
    mine_ref[...] = jnp.dot(chosen[...], mine, preferred_element_type=jnp.float32).astype(mine_ref.dtype)


def pick_own(core, features, lists, block_rows, block_cols, block_count):
    cap, owners = lists.shape
    rows, half = features.shape[0], features.shape[1] // 2
    anywhere = pl.BlockSpec(memory_space=pltpu.VMEM)
    return pl.pallas_call(
        pick_kernel,
        out_shape=(
            jax.ShapeDtypeStruct((owners * cap, half), features.dtype),
            jax.ShapeDtypeStruct((owners * cap + rows + cap, half), features.dtype),
        ),
        in_specs=[pl.BlockSpec(memory_space=pltpu.SMEM)] + [anywhere] * 5,
        out_specs=(anywhere, anywhere),
        scratch_shapes=[
            pltpu.VMEM((owners * cap, rows), jnp.bfloat16),
            pltpu.VMEM((cap, half), jnp.int32),
        ],
        compiler_params=pltpu.CompilerParams(vmem_limit_bytes=VMEM_BYTES),
    )(core.reshape(1), features, lists, block_rows, block_cols, block_count)


def finish_kernel(core_ref, first_ref, second_ref, others_ref, out_first_ref, out_second_ref):
    rows, half = others_ref.shape[1], others_ref.shape[2]
    core = core_ref[0]
    here = pl.ds(pl.multiple_of(core * half, half), half)
    there = pl.ds(pl.multiple_of((1 - core) * half, half), half)
    for place, (ref, out_ref) in enumerate(((first_ref, out_first_ref), (second_ref, out_second_ref))):
        out_ref[:, here] = ref[pl.ds(0, rows), :]
        out_ref[:, there] = others_ref[place]


def finish(core, first, second, others):
    anywhere = pl.BlockSpec(memory_space=pltpu.VMEM)
    shape = jax.ShapeDtypeStruct((others.shape[1], 2 * others.shape[2]), first.dtype)
    return pl.pallas_call(
        finish_kernel,
        out_shape=(shape, shape),
        in_specs=[pl.BlockSpec(memory_space=pltpu.SMEM)] + [anywhere] * 3,
        out_specs=(anywhere, anywhere),
        compiler_params=pltpu.CompilerParams(vmem_limit_bytes=VMEM_BYTES),
    )(core.reshape(1), first, second, others)


def one_hot(wanted, extent):
    place = lax.broadcasted_iota(jnp.int32, (1, extent), 1)
    return (wanted.reshape(-1, 1) == place).astype(jnp.bfloat16)


def on_device(features, blocks, block_rows, block_cols, block_count, send_rows):
    held = blocks[0]
    slots, tile = held.shape[0], held.shape[1]
    rows, width = features.shape
    half = width // 2
    cap = send_rows.shape[2]
    along, across = lax.axis_size("x"), lax.axis_size("z")
    owners = along * across
    slab_tiles = 2 * lax.axis_size("y")
    core = lax.axis_index("core")

    def swap(value):
        return lax.ppermute(value, "core", PAIR)

    def exchange(picked, axes=("x", "z")):
        got = lax.all_to_all(picked.reshape(lax.axis_size(axes), -1, half), axes, 0, 0, tiled=True)
        return got.reshape(-1, half)

    def pick(chosen, field):
        return jnp.dot(chosen, field, preferred_element_type=jnp.bfloat16)

    other_held = swap(held)
    lists = send_rows[0].T
    picked, sent = pick_own(core, features, lists, block_rows, block_cols, block_count)
    given = swap(sent)
    mine = jnp.where(core == 0, features[:, :half], features[:, half:])
    ends = owners * cap, owners * cap + rows

    def places(given):
        numbers = given[ends[1] :].astype(jnp.int32)
        other = [numbers[:1, rows : rows + slots], numbers[1:2, rows : rows + slots], numbers[2:3, rows : rows + 1]]
        meta = jnp.concatenate([jnp.concatenate([block_rows, block_cols, block_count], 1), jnp.concatenate(other, 1)], 0)
        is_row = lax.broadcasted_iota(jnp.int32, meta.shape, 1) < slots
        meta = jnp.where(is_row, meta ^ core, meta)
        wanted = jnp.stack([lists, numbers[:, :owners] + rows])
        return meta, wanted.transpose(2, 0, 1).reshape(-1)

    def multiply(field, starts, fetched, order, meta, held, other_held):
        partial_value = product(meta, held, other_held, field, starts, fetched, order, slab_tiles, cap)
        return partial_value.reshape(-1, 2 * rows, half)

    def combine(partial_value):
        parts = lax.all_to_all(partial_value, "y", 0, 0, tiled=True)
        return jnp.sum(parts.astype(jnp.float32), 0).astype(jnp.bfloat16)

    straight = tuple(range(owners))
    turned = tuple(q % across * along + q // across for q in straight)

    def in_one(operands):
        mine, picked, given, *tiles = operands
        meta, wanted = places(given)
        fetched = exchange(mix(picked, given, cap))
        partial_value = multiply((mine, given), (0, ends[0]), fetched, straight, meta, *tiles)
        partial_value, wanted = lax.optimization_barrier((partial_value, wanted))
        return combine(partial_value), meta, wanted

    def in_steps(operands):
        mine, picked, given, *tiles = operands
        meta, wanted = places(given)
        meta, wanted, picked, given = lax.optimization_barrier((meta, wanted, picked, given))
        shape = along, across, cap, half
        moved = [exchange(v, "x").reshape(shape) for v in (picked, given[: ends[0]])]
        fetched = exchange(jnp.stack(moved, 2).transpose(1, 0, 2, 3, 4), "z")
        partial_value = multiply((mine, given), (0, ends[0]), fetched, turned, meta, *tiles)
        return combine(partial_value), meta, wanted

    first, meta, wanted = lax.optimization_barrier(
        lax.cond(core == 0, in_one, in_steps, (mine, picked, given, held, other_held))
    )
    fetched = exchange(pick(one_hot(wanted, 2 * rows), first))
    second = combine(multiply((first,), (0,), fetched, straight, meta, held, other_held))
    kept_back = lax.optimization_barrier((first, second))
    others = swap(jnp.stack([v[rows:] for v in kept_back]))
    return finish(core, first, second, others)


def solution(mesh):
    inner = Mesh(
        mesh.devices.reshape(ALONG_X, mesh.shape["rows"] // ALONG_X, -1, 2), ("x", "z", "y", "core")
    )
    lines, cols = ("x", "z"), ("y", "core")
    placed = (
        P((*lines, *cols), None),
        P(lines, cols, None, None),
        P(lines, cols),
        P(lines, cols),
        P(lines, cols),
        P(lines, cols, None),
    )
    return jax.shard_map(
        on_device,
        mesh=inner,
        in_specs=placed,
        out_specs=(P((*lines, *cols), None), P((*lines, *cols), None)),
        check_vma=False,
    )
```

```python
import functools

import jax
import jax.numpy as jnp
from jax import lax
from jax.experimental import pallas as pl
from jax.experimental.pallas import tpu as pltpu
from jax.sharding import Mesh, PartitionSpec as P

GRP = 16
ALONG_X = 4
PAIR = [(0, 1), (1, 0)]
VMEM_BYTES = 16 * 1024 * 1024


def product_kernel(slots, cap, starts, order, meta_ref, own_ref, other_ref, *refs):
    field = refs[: len(starts)]
    fetched, out_ref, total, space = refs[len(starts) :]
    tile = own_ref.shape[1]
    tiles = space.shape[0] // 2
    for side in range(2):
        if len(field) == 2:
            space[side * tiles] = field[side][pl.ds(starts[side], tile), :]
        else:
            space[side * tiles] = field[0][pl.ds(side * tile, tile), :]
        for t in range(tiles - 1):
            for place in range(tile // cap):
                source = 2 * order[t * (tile // cap) + place] + side
                space[side * tiles + 1 + t, pl.ds(place * cap, cap), :] = fetched[
                    pl.ds(source * cap, cap), :
                ]
    total[...] = jnp.zeros_like(total)
    for side, ref in enumerate((own_ref, other_ref)):
        count = meta_ref[side, 2 * slots]

        def group(index, carry, side=side, ref=ref, count=count):
            products = []
            for step in range(GRP):
                k = index * GRP + step
                held = jnp.where(k < count, ref[k], jnp.zeros((tile, tile), ref.dtype))
                source = space[side * tiles + meta_ref[side, slots + k]]
                product = jnp.dot(held, source, preferred_element_type=jnp.float32)
                products.append((meta_ref[side, k], product))
            for row, product in products:
                total[row] += product
            return carry

        lax.fori_loop(0, (count + GRP - 1) // GRP, group, 0)
    for row in range(total.shape[0]):
        out_ref[pl.ds(row * tile, tile), :] = total[row].astype(out_ref.dtype)


def product(meta, own, other, field, starts, fetched, order, slab_tiles, cap):
    slots, tile = own.shape[0], own.shape[1]
    width = field[0].shape[1]
    tiles = 2 + fetched.shape[0] // tile
    anywhere = pl.BlockSpec(memory_space=pltpu.VMEM)
    return pl.pallas_call(
        functools.partial(product_kernel, slots, cap, starts, order),
        out_shape=jax.ShapeDtypeStruct((slab_tiles * tile, width), jnp.bfloat16),
        in_specs=[pl.BlockSpec(memory_space=pltpu.SMEM)] + [anywhere] * (3 + len(field)),
        out_specs=anywhere,
        scratch_shapes=[
            pltpu.VMEM((slab_tiles, tile, width), jnp.float32),
            pltpu.VMEM((tiles, tile, width), jnp.bfloat16),
        ],
        compiler_params=pltpu.CompilerParams(vmem_limit_bytes=VMEM_BYTES),
        cost_estimate=pl.CostEstimate(
            flops=4 * slots * tile * tile * width,
            bytes_accessed=2 * (2 * slots * tile * tile + (tiles + slab_tiles) * tile * width),
            transcendentals=0,
        ),
    )(meta, own, other, *field, fetched)


def mix_kernel(cap, mine_ref, given_ref, out_ref):
    for owner in range(mine_ref.shape[0] // cap):
        rows = pl.ds(owner * cap, cap)
        out_ref[pl.ds(2 * owner * cap, cap), :] = mine_ref[rows, :]
        out_ref[pl.ds((2 * owner + 1) * cap, cap), :] = given_ref[rows, :]


def mix(mine, given, cap):
    anywhere = pl.BlockSpec(memory_space=pltpu.VMEM)
    return pl.pallas_call(
        functools.partial(mix_kernel, cap),
        out_shape=jax.ShapeDtypeStruct((2 * mine.shape[0], mine.shape[1]), mine.dtype),
        in_specs=[anywhere, anywhere],
        out_specs=anywhere,
        compiler_params=pltpu.CompilerParams(vmem_limit_bytes=VMEM_BYTES),
    )(mine, given)


def pick_kernel(core_ref, features_ref, lists_ref, rows_ref, cols_ref, count_ref, mine_ref, sent_ref, chosen, numbers):
    cap, owners = lists_ref.shape
    rows, half = features_ref.shape[0], mine_ref.shape[1]
    place = lax.broadcasted_iota(jnp.int32, (cap, rows), 1)
    for owner in range(owners):
        wanted = lists_ref[:, pl.ds(owner, 1)]
        chosen[pl.ds(owner * cap, cap), :] = jnp.where(wanted == place, 1.0, 0.0).astype(chosen.dtype)
    core = core_ref[0]
    mine = features_ref[:, pl.ds(pl.multiple_of(core * half, half), half)]
    theirs = features_ref[:, pl.ds(pl.multiple_of((1 - core) * half, half), half)]
    ends = mine_ref.shape[0], mine_ref.shape[0] + rows
    sent_ref[pl.ds(0, ends[0]), :] = jnp.dot(
        chosen[...], theirs, preferred_element_type=jnp.float32
    ).astype(sent_ref.dtype)
    sent_ref[pl.ds(ends[0], rows), :] = theirs
    numbers[...] = jnp.zeros_like(numbers)
    numbers[:, pl.ds(0, owners)] = lists_ref[...]
    slots = rows_ref.shape[1]
    numbers[pl.ds(0, 1), pl.ds(rows, slots)] = rows_ref[...]
    numbers[pl.ds(1, 1), pl.ds(rows, slots)] = cols_ref[...]
    numbers[pl.ds(2, 1), pl.ds(rows, 1)] = count_ref[...]
    sent_ref[pl.ds(ends[1], cap), :] = numbers[...].astype(jnp.float32).astype(sent_ref.dtype)
    mine_ref[...] = jnp.dot(chosen[...], mine, preferred_element_type=jnp.float32).astype(mine_ref.dtype)


def pick_own(core, features, lists, block_rows, block_cols, block_count):
    cap, owners = lists.shape
    rows, half = features.shape[0], features.shape[1] // 2
    anywhere = pl.BlockSpec(memory_space=pltpu.VMEM)
    return pl.pallas_call(
        pick_kernel,
        out_shape=(
            jax.ShapeDtypeStruct((owners * cap, half), features.dtype),
            jax.ShapeDtypeStruct((owners * cap + rows + cap, half), features.dtype),
        ),
        in_specs=[pl.BlockSpec(memory_space=pltpu.SMEM)] + [anywhere] * 5,
        out_specs=(anywhere, anywhere),
        scratch_shapes=[
            pltpu.VMEM((owners * cap, rows), jnp.bfloat16),
            pltpu.VMEM((cap, half), jnp.int32),
        ],
        compiler_params=pltpu.CompilerParams(vmem_limit_bytes=VMEM_BYTES),
    )(core.reshape(1), features, lists, block_rows, block_cols, block_count)


def finish_kernel(core_ref, first_ref, second_ref, others_ref, out_first_ref, out_second_ref):
    rows, half = others_ref.shape[1], others_ref.shape[2]
    core = core_ref[0]
    here = pl.ds(pl.multiple_of(core * half, half), half)
    there = pl.ds(pl.multiple_of((1 - core) * half, half), half)
    for place, (ref, out_ref) in enumerate(((first_ref, out_first_ref), (second_ref, out_second_ref))):
        out_ref[:, here] = ref[pl.ds(0, rows), :]
        out_ref[:, there] = others_ref[place]


def finish(core, first, second, others):
    anywhere = pl.BlockSpec(memory_space=pltpu.VMEM)
    shape = jax.ShapeDtypeStruct((others.shape[1], 2 * others.shape[2]), first.dtype)
    return pl.pallas_call(
        finish_kernel,
        out_shape=(shape, shape),
        in_specs=[pl.BlockSpec(memory_space=pltpu.SMEM)] + [anywhere] * 3,
        out_specs=(anywhere, anywhere),
        compiler_params=pltpu.CompilerParams(vmem_limit_bytes=VMEM_BYTES),
    )(core.reshape(1), first, second, others)


def one_hot(wanted, extent):
    place = lax.broadcasted_iota(jnp.int32, (1, extent), 1)
    return (wanted.reshape(-1, 1) == place).astype(jnp.bfloat16)


def on_device(features, blocks, block_rows, block_cols, block_count, send_rows):
    held = blocks[0]
    slots, tile = held.shape[0], held.shape[1]
    rows, width = features.shape
    half = width // 2
    cap = send_rows.shape[2]
    along, across = lax.axis_size("x"), lax.axis_size("z")
    owners = along * across
    slab_tiles = 2 * lax.axis_size("y")
    core = lax.axis_index("core")

    def swap(value):
        return lax.ppermute(value, "core", PAIR)

    def exchange(picked, axes=("x", "z")):
        got = lax.all_to_all(picked.reshape(lax.axis_size(axes), -1, half), axes, 0, 0, tiled=True)
        return got.reshape(-1, half)

    def pick(chosen, field):
        return jnp.dot(chosen, field, preferred_element_type=jnp.bfloat16)

    other_held = swap(held)
    lists = send_rows[0].T
    picked, sent = pick_own(core, features, lists, block_rows, block_cols, block_count)
    given = swap(sent)
    mine = jnp.where(core == 0, features[:, :half], features[:, half:])
    ends = owners * cap, owners * cap + rows

    def places(given):
        numbers = given[ends[1] :].astype(jnp.int32)
        other = [numbers[:1, rows : rows + slots], numbers[1:2, rows : rows + slots], numbers[2:3, rows : rows + 1]]
        meta = jnp.concatenate([jnp.concatenate([block_rows, block_cols, block_count], 1), jnp.concatenate(other, 1)], 0)
        is_row = lax.broadcasted_iota(jnp.int32, meta.shape, 1) < slots
        meta = jnp.where(is_row, meta ^ core, meta)
        wanted = jnp.stack([lists, numbers[:, :owners] + rows])
        return meta, wanted.transpose(2, 0, 1).reshape(-1)

    def multiply(field, starts, fetched, order, meta, held, other_held):
        partial_value = product(meta, held, other_held, field, starts, fetched, order, slab_tiles, cap)
        return partial_value.reshape(-1, 2 * rows, half)

    def combine(partial_value):
        parts = lax.all_to_all(partial_value, "y", 0, 0, tiled=True)
        return jnp.sum(parts.astype(jnp.float32), 0).astype(jnp.bfloat16)

    straight = tuple(range(owners))
    turned = tuple(q % across * along + q // across for q in straight)

    def in_one(operands):
        mine, picked, given, *tiles = operands
        meta, wanted = places(given)
        fetched = exchange(mix(picked, given, cap))
        partial_value = multiply((mine, given), (0, ends[0]), fetched, straight, meta, *tiles)
        partial_value, wanted = lax.optimization_barrier((partial_value, wanted))
        return combine(partial_value), meta, wanted

    def in_steps(operands):
        mine, picked, given, *tiles = operands
        meta, wanted = places(given)
        meta, wanted, picked, given = lax.optimization_barrier((meta, wanted, picked, given))
        shape = along, across, cap, half
        moved = [exchange(v, "x").reshape(shape) for v in (picked, given[: ends[0]])]
        fetched = exchange(jnp.stack(moved, 2).transpose(1, 0, 2, 3, 4), "z")
        partial_value = multiply((mine, given), (0, ends[0]), fetched, turned, meta, *tiles)
        return combine(partial_value), meta, wanted

    first, meta, wanted = lax.optimization_barrier(
        lax.cond(core == 0, in_one, in_steps, (mine, picked, given, held, other_held))
    )
    fetched = exchange(pick(one_hot(wanted, 2 * rows), first))
    second = combine(multiply((first,), (0,), fetched, straight, meta, held, other_held))
    kept_back = lax.optimization_barrier((first, second))
    others = swap(jnp.stack([v[rows:] for v in kept_back]))
    return finish(core, first, second, others)


def solution(mesh):
    inner = Mesh(
        mesh.devices.reshape(ALONG_X, mesh.shape["rows"] // ALONG_X, -1, 2), ("x", "z", "y", "core")
    )
    lines, cols = ("x", "z"), ("y", "core")
    placed = (
        P((*lines, *cols), None),
        P(lines, cols, None, None),
        P(lines, cols),
        P(lines, cols),
        P(lines, cols),
        P(lines, cols, None),
    )
    return jax.shard_map(
        on_device,
        mesh=inner,
        in_specs=placed,
        out_specs=(P((*lines, *cols), None), P((*lines, *cols), None)),
        check_vma=False,
    )
```

```python
import functools

import jax
import jax.numpy as jnp
from jax import lax
from jax.experimental import pallas as pl
from jax.experimental.pallas import tpu as pltpu
from jax.sharding import Mesh, PartitionSpec as P

GRP = 16
ALONG_X = 4
PAIR = [(0, 1), (1, 0)]
VMEM_BYTES = 16 * 1024 * 1024


def product_kernel(slots, cap, starts, order, meta_ref, own_ref, other_ref, *refs):
    field = refs[: len(starts)]
    fetched, out_ref, total, space = refs[len(starts) :]
    tile = own_ref.shape[1]
    tiles = space.shape[0] // 2
    for side in range(2):
        if len(field) == 2:
            space[side * tiles] = field[side][pl.ds(starts[side], tile), :]
        else:
            space[side * tiles] = field[0][pl.ds(side * tile, tile), :]
        for t in range(tiles - 1):
            for place in range(tile // cap):
                source = 2 * order[t * (tile // cap) + place] + side
                space[side * tiles + 1 + t, pl.ds(place * cap, cap), :] = fetched[
                    pl.ds(source * cap, cap), :
                ]
    total[...] = jnp.zeros_like(total)
    for side, ref in enumerate((own_ref, other_ref)):
        count = meta_ref[side, 2 * slots]

        def group(index, carry, side=side, ref=ref, count=count):
            products = []
            for step in range(GRP):
                k = index * GRP + step
                held = jnp.where(k < count, ref[k], jnp.zeros((tile, tile), ref.dtype))
                source = space[side * tiles + meta_ref[side, slots + k]]
                product = jnp.dot(held, source, preferred_element_type=jnp.float32)
                products.append((meta_ref[side, k], product))
            for row, product in products:
                total[row] += product
            return carry

        lax.fori_loop(0, (count + GRP - 1) // GRP, group, 0)
    for row in range(total.shape[0]):
        out_ref[pl.ds(row * tile, tile), :] = total[row].astype(out_ref.dtype)


def product(meta, own, other, field, starts, fetched, order, slab_tiles, cap):
    slots, tile = own.shape[0], own.shape[1]
    width = field[0].shape[1]
    tiles = 2 + fetched.shape[0] // tile
    anywhere = pl.BlockSpec(memory_space=pltpu.VMEM)
    return pl.pallas_call(
        functools.partial(product_kernel, slots, cap, starts, order),
        out_shape=jax.ShapeDtypeStruct((slab_tiles * tile, width), jnp.bfloat16),
        in_specs=[pl.BlockSpec(memory_space=pltpu.SMEM)] + [anywhere] * (3 + len(field)),
        out_specs=anywhere,
        scratch_shapes=[
            pltpu.VMEM((slab_tiles, tile, width), jnp.float32),
            pltpu.VMEM((tiles, tile, width), jnp.bfloat16),
        ],
        compiler_params=pltpu.CompilerParams(vmem_limit_bytes=VMEM_BYTES),
        cost_estimate=pl.CostEstimate(
            flops=4 * slots * tile * tile * width,
            bytes_accessed=2 * (2 * slots * tile * tile + (tiles + slab_tiles) * tile * width),
            transcendentals=0,
        ),
    )(meta, own, other, *field, fetched)


def mix_kernel(cap, mine_ref, given_ref, out_ref):
    for owner in range(mine_ref.shape[0] // cap):
        rows = pl.ds(owner * cap, cap)
        out_ref[pl.ds(2 * owner * cap, cap), :] = mine_ref[rows, :]
        out_ref[pl.ds((2 * owner + 1) * cap, cap), :] = given_ref[rows, :]


def mix(mine, given, cap):
    anywhere = pl.BlockSpec(memory_space=pltpu.VMEM)
    return pl.pallas_call(
        functools.partial(mix_kernel, cap),
        out_shape=jax.ShapeDtypeStruct((2 * mine.shape[0], mine.shape[1]), mine.dtype),
        in_specs=[anywhere, anywhere],
        out_specs=anywhere,
        compiler_params=pltpu.CompilerParams(vmem_limit_bytes=VMEM_BYTES),
    )(mine, given)


def pick_kernel(core_ref, features_ref, lists_ref, rows_ref, cols_ref, count_ref, own_ref, mine_ref, sent_ref, chosen, numbers):
    cap, owners = lists_ref.shape
    rows, half = features_ref.shape[0], mine_ref.shape[1]
    place = lax.broadcasted_iota(jnp.int32, (cap, rows), 1)
    for owner in range(owners):
        wanted = lists_ref[:, pl.ds(owner, 1)]
        chosen[pl.ds(owner * cap, cap), :] = jnp.where(wanted == place, 1.0, 0.0).astype(chosen.dtype)
    core = core_ref[0]
    mine = features_ref[:, pl.ds(pl.multiple_of(core * half, half), half)]
    theirs = features_ref[:, pl.ds(pl.multiple_of((1 - core) * half, half), half)]
    ends = mine_ref.shape[0], mine_ref.shape[0] + rows
    sent_ref[pl.ds(0, ends[0]), :] = jnp.dot(
        chosen[...], theirs, preferred_element_type=jnp.float32
    ).astype(sent_ref.dtype)
    sent_ref[pl.ds(ends[0], rows), :] = theirs
    numbers[...] = jnp.zeros_like(numbers)
    numbers[:, pl.ds(0, owners)] = lists_ref[...]
    slots = rows_ref.shape[1]
    numbers[pl.ds(0, 1), pl.ds(rows, slots)] = rows_ref[...]
    numbers[pl.ds(1, 1), pl.ds(rows, slots)] = cols_ref[...]
    numbers[pl.ds(2, 1), pl.ds(rows, 1)] = count_ref[...]
    sent_ref[pl.ds(ends[1], cap), :] = numbers[...].astype(jnp.float32).astype(sent_ref.dtype)
    own_ref[...] = mine
    mine_ref[...] = jnp.dot(chosen[...], mine, preferred_element_type=jnp.float32).astype(mine_ref.dtype)


def pick_own(core, features, lists, block_rows, block_cols, block_count):
    cap, owners = lists.shape
    rows, half = features.shape[0], features.shape[1] // 2
    anywhere = pl.BlockSpec(memory_space=pltpu.VMEM)
    return pl.pallas_call(
        pick_kernel,
        out_shape=(
            jax.ShapeDtypeStruct((rows, half), features.dtype),
            jax.ShapeDtypeStruct((owners * cap, half), features.dtype),
            jax.ShapeDtypeStruct((owners * cap + rows + cap, half), features.dtype),
        ),
        in_specs=[pl.BlockSpec(memory_space=pltpu.SMEM)] + [anywhere] * 5,
        out_specs=(anywhere, anywhere, anywhere),
        scratch_shapes=[
            pltpu.VMEM((owners * cap, rows), jnp.bfloat16),
            pltpu.VMEM((cap, half), jnp.int32),
        ],
        compiler_params=pltpu.CompilerParams(vmem_limit_bytes=VMEM_BYTES),
    )(core.reshape(1), features, lists, block_rows, block_cols, block_count)


def finish_kernel(core_ref, first_ref, second_ref, others_ref, out_first_ref, out_second_ref):
    rows, half = others_ref.shape[1], others_ref.shape[2]
    core = core_ref[0]
    here = pl.ds(pl.multiple_of(core * half, half), half)
    there = pl.ds(pl.multiple_of((1 - core) * half, half), half)
    for place, (ref, out_ref) in enumerate(((first_ref, out_first_ref), (second_ref, out_second_ref))):
        out_ref[:, here] = ref[pl.ds(0, rows), :]
        out_ref[:, there] = others_ref[place]


def finish(core, first, second, others):
    anywhere = pl.BlockSpec(memory_space=pltpu.VMEM)
    shape = jax.ShapeDtypeStruct((others.shape[1], 2 * others.shape[2]), first.dtype)
    return pl.pallas_call(
        finish_kernel,
        out_shape=(shape, shape),
        in_specs=[pl.BlockSpec(memory_space=pltpu.SMEM)] + [anywhere] * 3,
        out_specs=(anywhere, anywhere),
        compiler_params=pltpu.CompilerParams(vmem_limit_bytes=VMEM_BYTES),
    )(core.reshape(1), first, second, others)


def one_hot(wanted, extent):
    place = lax.broadcasted_iota(jnp.int32, (1, extent), 1)
    return (wanted.reshape(-1, 1) == place).astype(jnp.bfloat16)


def on_device(features, blocks, block_rows, block_cols, block_count, send_rows):
    held = blocks[0]
    slots, tile = held.shape[0], held.shape[1]
    rows, width = features.shape
    half = width // 2
    cap = send_rows.shape[2]
    along, across = lax.axis_size("x"), lax.axis_size("z")
    owners = along * across
    slab_tiles = 2 * lax.axis_size("y")
    core = lax.axis_index("core")

    def swap(value):
        return lax.ppermute(value, "core", PAIR)

    def exchange(picked, axes=("x", "z")):
        got = lax.all_to_all(picked.reshape(lax.axis_size(axes), -1, half), axes, 0, 0, tiled=True)
        return got.reshape(-1, half)

    def pick(chosen, field):
        return jnp.dot(chosen, field, preferred_element_type=jnp.bfloat16)

    other_held = swap(held)
    lists = send_rows[0].T
    mine, picked, sent = pick_own(core, features, lists, block_rows, block_cols, block_count)
    given = swap(sent)
    ends = owners * cap, owners * cap + rows

    def places(given):
        numbers = given[ends[1] :].astype(jnp.int32)
        other = [numbers[:1, rows : rows + slots], numbers[1:2, rows : rows + slots], numbers[2:3, rows : rows + 1]]
        meta = jnp.concatenate([jnp.concatenate([block_rows, block_cols, block_count], 1), jnp.concatenate(other, 1)], 0)
        is_row = lax.broadcasted_iota(jnp.int32, meta.shape, 1) < slots
        meta = jnp.where(is_row, meta ^ core, meta)
        wanted = jnp.stack([lists, numbers[:, :owners] + rows])
        return meta, wanted.transpose(2, 0, 1).reshape(-1)

    def multiply(field, starts, fetched, order, meta, held, other_held):
        partial_value = product(meta, held, other_held, field, starts, fetched, order, slab_tiles, cap)
        return partial_value.reshape(-1, 2 * rows, half)

    def combine(partial_value):
        parts = lax.all_to_all(partial_value, "y", 0, 0, tiled=True)
        return jnp.sum(parts.astype(jnp.float32), 0).astype(jnp.bfloat16)

    straight = tuple(range(owners))
    turned = tuple(q % across * along + q // across for q in straight)

    def in_one(operands):
        mine, picked, given, *tiles = operands
        meta, wanted = places(given)
        fetched = exchange(mix(picked, given, cap))
        partial_value = multiply((mine, given), (0, ends[0]), fetched, straight, meta, *tiles)
        partial_value, wanted = lax.optimization_barrier((partial_value, wanted))
        return combine(partial_value), meta, wanted

    def in_steps(operands):
        mine, picked, given, *tiles = operands
        meta, wanted = places(given)
        meta, wanted, picked, given = lax.optimization_barrier((meta, wanted, picked, given))
        shape = along, across, cap, half
        moved = [exchange(v, "x").reshape(shape) for v in (picked, given[: ends[0]])]
        fetched = exchange(jnp.stack(moved, 2).transpose(1, 0, 2, 3, 4), "z")
        partial_value = multiply((mine, given), (0, ends[0]), fetched, turned, meta, *tiles)
        return combine(partial_value), meta, wanted

    first, meta, wanted = lax.optimization_barrier(
        lax.cond(core == 0, in_one, in_steps, (mine, picked, given, held, other_held))
    )
    fetched = exchange(pick(one_hot(wanted, 2 * rows), first))
    second = combine(multiply((first,), (0,), fetched, straight, meta, held, other_held))
    kept_back = lax.optimization_barrier((first, second))
    others = swap(jnp.stack([v[rows:] for v in kept_back]))
    return finish(core, first, second, others)


def solution(mesh):
    inner = Mesh(
        mesh.devices.reshape(ALONG_X, mesh.shape["rows"] // ALONG_X, -1, 2), ("x", "z", "y", "core")
    )
    lines, cols = ("x", "z"), ("y", "core")
    placed = (
        P((*lines, *cols), None),
        P(lines, cols, None, None),
        P(lines, cols),
        P(lines, cols),
        P(lines, cols),
        P(lines, cols, None),
    )
    return jax.shard_map(
        on_device,
        mesh=inner,
        in_specs=placed,
        out_specs=(P((*lines, *cols), None), P((*lines, *cols), None)),
        check_vma=False,
    )
```
